32 devices in a mesh: section: 4 (over y, x), tile: 8 (over z, core).
Axes of the slice: x: 2, y: 2, z: 4, core: 2. Of those that a mesh axis runs over, the one named last changes fastest.
Arguments:
- features: bfloat16 [32, 16, 16, 256], P('tile'), may hold values from -6 to 6
- out_cotangent: bfloat16 [32, 16, 16, 256], P('tile'), may hold values from -6 to 6
- w_reduce: bfloat16 [4, 256, 64], P('section'), may hold values from -0.375 to 0.375
- w_taps: bfloat16 [4, 576, 64], P('section'), may hold values from -0.25 to 0.25
- w_expand: bfloat16 [4, 64, 256], P('section'), may hold values from -0.75 to 0.75
- norm_scale: float32 [4, 384], P('section'), may hold values from 0.25 to 1.75
- norm_shift: float32 [4, 384], P('section'), may hold values from -2 to 2
- owner: int32 [32], replicated, may hold values from 0 to 31, as said below
- neighbours: int32 [32, 4], replicated, may hold values from -1 to 31, as said below
Outputs:
- block_outputs: bfloat16 [4, 32, 16, 16, 256], P('section', 'tile')
- input_grads: bfloat16 [4, 32, 16, 16, 256], P('section', 'tile')
- grad_reduce: float32 [4, 256, 64], P('section')
- grad_taps: float32 [4, 576, 64], P('section')
- grad_expand: float32 [4, 64, 256], P('section')
The draws below stay inside these ranges and needn't reach their ends.
Inputs may be any that keep to these rules, and one draw needn't show every extreme that they name: `owner`: A permutation of the rows; the rows 4 k to 4 k + 3 belong to index k of tile. The tiles form a band 8 tiles across; two neighbouring tiles are owned by indices of tile at most 3 apart, and west and east neighbours by indices at most 1 apart. Symmetric: if neighbours[t, 0] = u then neighbours[u, 1] = t, and likewise for west and east; -1 at the band's border.
All inputs are finite; a program needn't handle non-finite values.
Results may differ from the reference program's by a relative error of at most 0.039.
Values may be sent and summed in bfloat16 or wider, within the bound.
A program may use at most 64 MiB of HBM per device.

```python
import jax
import jax.numpy as jnp
import numpy as np
from jax import lax

C = 256
M = 64
P_SIZE = 16
TILE_DEV = 4
BLOCKS = 4
BAND_W = 8
TILES = 32
NORM = 384


def band_layout(key):
    key_ids = jax.random.fold_in(key, 101)
    key_mix = jax.random.fold_in(key, 202)
    ids = jax.random.permutation(key_ids, TILES).astype(jnp.int32)
    group = 2 * TILE_DEV
    groups = TILES // group
    scores = jax.random.randint(key_mix, (groups, group), 0, 1 << 20).astype(jnp.int32) * group
    scores = scores + jnp.arange(group, dtype=jnp.int32)[None, :]
    within = jnp.argsort(scores, axis=1).astype(jnp.int32)
    slot_of_pos = (jnp.arange(groups, dtype=jnp.int32)[:, None] * group + within).reshape(-1)
    position = jnp.arange(TILES, dtype=jnp.int32)
    row = position // BAND_W
    col = position % BAND_W
    rows = TILES // BAND_W
    north = jnp.where(row > 0, position - BAND_W, -1)
    south = jnp.where(row < rows - 1, position + BAND_W, -1)
    west = jnp.where(col > 0, position - 1, -1)
    east = jnp.where(col < BAND_W - 1, position + 1, -1)
    near_pos = jnp.stack([north, south, west, east], axis=1)
    near_ids = jnp.where(near_pos >= 0, jnp.take(ids, jnp.maximum(near_pos, 0)), -1).astype(jnp.int32)
    owner = jnp.zeros((TILES,), jnp.int32).at[ids].set(slot_of_pos)
    neighbours = jnp.zeros((TILES, 4), jnp.int32).at[ids].set(near_ids)
    return (owner, neighbours)


def draw_owner(key, part):
    return band_layout(key)[0]


def draw_neighbours(key, part):
    return band_layout(key)[1]


def raised(entries, own_key, source, target, blocks, factor):
    def block_of(axis_at):
        return (jnp.arange(entries.shape[axis_at]) // (entries.shape[axis_at] // blocks)).reshape((-1,) + (1,) * (entries.ndim - 1 - axis_at))

    first = jax.random.permutation(own_key, blocks)[block_of(target)]
    second = (block_of(target) + blocks // 2) % blocks
    return jnp.where((block_of(source) == first) | (block_of(source) == second), factor * entries, entries)


def steps_of(rng, dims, cuts, smallest, top_value):
    level, own = 1.0, jax.random.fold_in(rng, 6)
    for dim, blocks in cuts:
        draws = jnp.exp(jax.random.uniform(jax.random.fold_in(own, dim), (blocks,), jnp.float32, smallest / len(cuts), top_value / len(cuts)))
        level = level * jnp.repeat(draws, dims[dim] // blocks).reshape([-1 if axis == dim else 1 for axis in range(len(dims))])
    return level


def bell_draw(own_key, shape, deviation, most, cuts=(), kind=jnp.bfloat16):
    values = jax.random.normal(own_key, shape, jnp.float32) * deviation
    if len(cuts) > 0:
        values = steps_of(own_key, shape, cuts, -0.22, 0.18) * values
    return jnp.clip(values, min=-most, max=most).astype(kind)


def noise_with(own_key, shape, spread, reach, cuts, heavy, held_as=jnp.bfloat16):
    values = spread * jax.random.normal(own_key, shape, jnp.float32)
    if cuts:
        values = values * steps_of(own_key, shape, cuts, -0.22, 0.18)
    return jnp.clip(raised(values, jax.random.fold_in(own_key, 3), *heavy), -reach, reach).astype(held_as)


def setup_inputs(seed: int = 0) -> dict:
    splits = jax.random.split(jax.random.key(seed), 10)
    features = bell_draw(splits[0], (TILES, P_SIZE, P_SIZE, C), 1.0, 6.0, ((0, 8),))
    out_cotangent = noise_with(splits[1], (TILES, P_SIZE, P_SIZE, C), 1.0, 6.0, ((0, 8),), (0, 3, 8, 2.0))
    w_reduce = bell_draw(splits[2], (BLOCKS, C, M), C ** -0.5, 0.375, ((0, 4),))
    w_taps = bell_draw(splits[3], (BLOCKS, 9 * M, M), (9 * M) ** -0.5, 0.25, ((0, 4),))
    w_expand = bell_draw(splits[4], (BLOCKS, M, C), M ** -0.5, 0.75, ((0, 4),))
    norm_scale = jnp.clip(1.0 + 0.15 * jax.random.normal(splits[5], (BLOCKS, NORM), jnp.float32), 0.25, 1.75)
    norm_shift = bell_draw(splits[6], (BLOCKS, NORM), 0.3, 2.0, ((0, 4),), jnp.float32)
    owner = draw_owner(jax.random.fold_in(splits[9], 71), 0)
    neighbours = draw_neighbours(jax.random.fold_in(splits[9], 71), 0)
    return dict(features=features, out_cotangent=out_cotangent, w_reduce=w_reduce, w_taps=w_taps, w_expand=w_expand, norm_scale=norm_scale, norm_shift=norm_shift, owner=owner, neighbours=neighbours)


OPPOSITE = np.array([1, 0, 3, 2], dtype=np.int32)

def silu_grad(value):
    sig = jax.nn.sigmoid(value)
    return sig * (1.0 + value * (1.0 - sig))

def inner_product(left, right):
    return lax.dot_general(left, right, (((0,), (0,)), ((), ())), preferred_element_type=jnp.float32)

def times_transposed(left, right):
    return lax.dot_general(left, right, (((1,), (1,)), ((), ())), preferred_element_type=jnp.float32)

def face_targets(owner, neighbours, slots):
    tiles = owner.shape[0]
    hit = owner[None, :] == slots[:, None]
    tile_ids = lax.optimization_barrier(jnp.sum(jnp.where(hit, jnp.arange(tiles, dtype=jnp.int32)[None, :], 0), axis=1)).astype(jnp.int32)
    near = jnp.take(neighbours, tile_ids, axis=0)
    valid = near >= 0
    near_slot = jnp.take(owner, jnp.where(valid, near, 0), axis=0).astype(jnp.int32)
    return (near_slot, valid)

def edge_rows(field):
    count, side, _, width = field.shape
    rows = jnp.stack([field[:, 0], field[:, side - 1], field[:, :, 0], field[:, :, side - 1]], axis=1)
    return rows.reshape(count, 4, side * width)

def halo_rows(d_padded):
    count = d_padded.shape[0]
    width = d_padded.shape[3]
    side = d_padded.shape[1] - 2
    rows = jnp.stack([d_padded[:, 0, 1:-1], d_padded[:, -1, 1:-1], d_padded[:, 1:-1, 0], d_padded[:, 1:-1, -1]], axis=1)
    return rows.reshape(count, 4, side * width)

def with_faces(hidden, faces):
    count, side, _, width = hidden.shape
    faces = faces.reshape(count, 4, side, width)
    middle = jnp.concatenate([faces[:, 2][:, :, None], hidden, faces[:, 3][:, :, None]], axis=2)
    corner = jnp.zeros((count, 1, 1, width), hidden.dtype)
    top = jnp.concatenate([corner, faces[:, 0][:, None], corner], axis=2)
    bottom = jnp.concatenate([corner, faces[:, 1][:, None], corner], axis=2)
    return jnp.concatenate([top, middle, bottom], axis=1)

def reduce_front(inputs, w_red, scale, shift):
    count, side, _, chans = inputs.shape
    width = w_red.shape[1]
    pre1 = jnp.dot(inputs.reshape(-1, chans), w_red, preferred_element_type=jnp.float32) * scale[:width] + shift[:width]
    return (pre1, jax.nn.silu(pre1).astype(jnp.bfloat16).reshape(count, side, side, width))

def block_tail(inputs, padded, w_tap, w_exp, scale, shift):
    side = inputs.shape[1]
    chans = inputs.shape[3]
    width = w_tap.shape[1]
    parts = [padded[:, dy:dy + side, dx:dx + side, :] for dy in range(3) for dx in range(3)]
    columns = jnp.concatenate(parts, axis=-1).reshape(-1, 9 * width)
    pre2 = jnp.dot(columns, w_tap, preferred_element_type=jnp.float32) * scale[width:2 * width] + shift[width:2 * width]
    hidden2 = jax.nn.silu(pre2).astype(jnp.bfloat16)
    expanded = jnp.dot(hidden2, w_exp, preferred_element_type=jnp.float32)
    pre3 = inputs.reshape(-1, chans).astype(jnp.float32) + expanded * scale[2 * width:] + shift[2 * width:]
    return (columns, pre2, hidden2, pre3)

def block_forward(inputs, params, fetch):
    w_red, w_tap, w_exp, scale, shift = params
    pre1, hidden1 = reduce_front(inputs, w_red, scale, shift)
    padded = with_faces(hidden1, fetch(edge_rows(hidden1)))
    columns, pre2, hidden2, pre3 = block_tail(inputs, padded, w_tap, w_exp, scale, shift)
    return (jax.nn.silu(pre3).astype(jnp.bfloat16).reshape(inputs.shape), padded)

def block_backward(inputs, padded, upstream, params, fetch):
    w_red, w_tap, w_exp, scale, shift = params
    count, side, _, chans = inputs.shape
    width = w_tap.shape[1]
    pre1, hidden1 = reduce_front(inputs, w_red, scale, shift)
    columns, pre2, hidden2, pre3 = block_tail(inputs, padded, w_tap, w_exp, scale, shift)
    d_pre3 = upstream.reshape(pre3.shape).astype(jnp.float32) * silu_grad(pre3)
    e_three = (d_pre3 * scale[2 * width:]).astype(jnp.bfloat16)
    g_expand = inner_product(hidden2, e_three)
    d_two = (times_transposed(e_three, w_exp) * silu_grad(pre2) * scale[width:2 * width]).astype(jnp.bfloat16)
    g_taps = inner_product(columns, d_two)
    d_columns = times_transposed(d_two, w_tap).reshape(count, side, side, 9 * width)
    d_padded = jnp.zeros((count, side + 2, side + 2, width), jnp.float32)
    for tap in range(9):
        dy, dx = (tap // 3, tap % 3)
        piece = d_columns[..., tap * width:(tap + 1) * width]
        d_padded = d_padded + jnp.pad(piece, ((0, 0), (dy, 2 - dy), (dx, 2 - dx), (0, 0)))
    d_padded = d_padded.astype(jnp.bfloat16)
    received = fetch(halo_rows(d_padded)).reshape(count, 4, side, width).astype(jnp.float32)
    d_hidden = d_padded[:, 1:-1, 1:-1].astype(jnp.float32)
    d_hidden = d_hidden.at[:, 0].add(received[:, 0])
    d_hidden = d_hidden.at[:, side - 1].add(received[:, 1])
    d_hidden = d_hidden.at[:, :, 0].add(received[:, 2])
    d_hidden = d_hidden.at[:, :, side - 1].add(received[:, 3])
    d_one = (d_hidden.reshape(-1, width) * silu_grad(pre1) * scale[:width]).astype(jnp.bfloat16)
    g_reduce = inner_product(inputs.reshape(-1, chans), d_one)
    d_inputs = (d_pre3 + times_transposed(d_one, w_red)).astype(jnp.bfloat16).reshape(inputs.shape)
    return (d_inputs, (g_reduce, g_taps, g_expand))

def reference(features, out_cotangent, w_reduce, w_taps, w_expand, norm_scale, norm_shift, owner, neighbours):
    tiles = features.shape[0]
    blocks = w_reduce.shape[0]
    slots = jnp.arange(tiles, dtype=jnp.int32)
    near_slot, valid = face_targets(owner, neighbours, slots)
    place = jnp.where(valid, near_slot * 4 + OPPOSITE[None, :], 0).astype(jnp.int32)

    def fetch(edges):
        pool = edges.reshape(-1, edges.shape[-1])
        picked = jnp.take(pool, place.reshape(-1), axis=0).reshape(edges.shape)
        return jnp.where(valid[..., None], picked, jnp.zeros_like(picked))
    held = features
    inputs_list, pads, outs = ([], [], [])
    for step in range(blocks):
        params = (w_reduce[step], w_taps[step], w_expand[step], norm_scale[step], norm_shift[step])
        result, padded = block_forward(held, params, fetch)
        inputs_list.append(held)
        pads.append(padded)
        outs.append(result)
        held = result
    upstream = out_cotangent
    d_list = [None] * blocks
    g_lists = [None] * blocks
    for step in reversed(range(blocks)):
        params = (w_reduce[step], w_taps[step], w_expand[step], norm_scale[step], norm_shift[step])
        d_inputs, grads = block_backward(inputs_list[step], pads[step], upstream, params, fetch)
        d_list[step] = d_inputs
        g_lists[step] = grads
        upstream = d_inputs
    return (jnp.stack(outs), jnp.stack(d_list), jnp.stack([g[0] for g in g_lists]), jnp.stack([g[1] for g in g_lists]), jnp.stack([g[2] for g in g_lists]))
```

```python
from functools import partial

import jax
import jax.numpy as jnp
import numpy as np
from jax import lax
from jax.experimental import pallas as pl
from jax.experimental.pallas import tpu as pltpu
from jax.sharding import PartitionSpec as P

REACH = 3
SPAN = 2 * REACH + 1
MESH = pl.DeviceIdType.MESH
SIDE = 16
PIX = SIDE * SIDE
EXT = PIX + 2 * SIDE
FULL = EXT + 2 * SIDE
ROWS = 544


def shift_matrices():
    left = np.zeros((EXT, FULL), np.float32)
    right = np.zeros((EXT, FULL), np.float32)
    for r in range(EXT):
        y, x = r // SIDE - 1, r % SIDE
        inside = 0 <= y < SIDE
        if x > 0:
            left[r, r - 1] = 1
        elif inside:
            left[r, EXT + y] = 1
        if x < SIDE - 1:
            right[r, r + 1] = 1
        elif inside:
            right[r, EXT + SIDE + y] = 1
    face = np.zeros((4 * SIDE, PIX), np.float32)
    for i in range(SIDE):
        face[i, i] = 1
        face[SIDE + i, PIX - SIDE + i] = 1
        face[2 * SIDE + i, SIDE * i] = 1
        face[3 * SIDE + i, SIDE * i + SIDE - 1] = 1
    return np.concatenate([left, right]), face


def sigmoid(v):
    return 0.5 * jnp.tanh(0.5 * v) + 0.5


def mm(left, right):
    return jnp.dot(left, right, preferred_element_type=jnp.float32)


def mm_t(left, right):
    return lax.dot_general(
        left, right, (((1,), (1,)), ((), ())), preferred_element_type=jnp.float32
    )


def t_mm(left, right):
    return lax.dot_general(
        left, right, (((0,), (0,)), ((), ())), preferred_element_type=jnp.float32
    )


def kernel(
    n, blocks, chunk, owners,
    owner_ref, near_ref, feat_ref, cot_ref, w1_ref, wt_ref, w3_ref, sc_ref, sh_ref,
    shift_ref, shift_t_ref, face_ref, face_t_ref,
    out_ref, din_ref, gr_ref, gt_ref, ge_ref,
    sel, acts, cot, dins, W1, WT, W3, NS, NT,
    D1, D2, D3, pre2_s, pre3_s, CAT, H2, E3, DD3, F, SEND, RECV, HELD, G, GR, P2, FIN,
    load_sem, wl_sem, ws_sem, wr_sem, xs_sem, xr_sem,
    os_sem, or_sem, ol_sem, gs_sem, gr_sem, ps_sem, pr_sem, fs_sem, fr_sem,
):
    s = lax.axis_index("section")
    k = lax.axis_index("tile")
    lo = jnp.maximum(k - REACH, 0)
    hi = jnp.minimum(k + REACH + 1, n)
    bf = jnp.bfloat16

    feat_copy = pltpu.make_async_copy(feat_ref.at[s], acts.at[0], load_sem.at[0])
    cot_copy = pltpu.make_async_copy(cot_ref.at[s], cot, load_sem.at[1])
    feat_copy.start()
    cot_copy.start()
    weights = [
        (w1_ref.at[0], W1), (sc_ref, NS), (sh_ref, NT), (wt_ref.at[0], WT), (w3_ref.at[0], W3)
    ]
    for i, (src, dst) in enumerate(weights):
        pltpu.make_async_copy(src, dst.at[s], wl_sem.at[i]).start()

    barrier = pltpu.get_barrier_semaphore()

    def greet(kk, total):
        near = jnp.logical_and(kk >= lo, kk < hi)
        for ss in range(blocks):
            go = jnp.logical_and(
                jnp.logical_or(near, s == ss), jnp.logical_not(jnp.logical_and(s == ss, kk == k))
            )

            @pl.when(go)
            def _():
                pl.semaphore_signal(barrier, inc=1, device_id=(ss, kk), device_id_type=MESH)

        return total

    lax.fori_loop(0, n, greet, 0)
    pl.semaphore_wait(barrier, (hi - lo) * (blocks - 1) + n - 1)

    def weight_copy(i, target, slot):
        src, dst = weights[i]
        return pltpu.make_async_remote_copy(
            src_ref=src, dst_ref=dst.at[slot],
            send_sem=ws_sem.at[i, target], recv_sem=wr_sem.at[i, slot],
            device_id=(target, k), device_id_type=MESH,
        )

    for i in range(len(weights)):
        for target in range(blocks):
            @pl.when(s != target)
            def _():
                weight_copy(i, target, s).start()

    slot = k * blocks + s
    tiles = owner_ref.shape[0]
    tile = lax.fori_loop(
        0, tiles, lambda i, acc: jnp.where(owner_ref[i] == slot, i, acc), jnp.int32(0)
    )
    places, valids = [], []
    for j in range(4):
        near = near_ref[tile * 4 + j]
        valid = near >= 0
        where = owner_ref[jnp.where(valid, near, 0)]
        place = (where // blocks - k + REACH) * blocks + where % blocks
        place = jnp.where(valid, place, 0)
        places.append(jnp.clip(place, 0, SPAN * blocks - 1))
        valids.append(valid)
    for i in range(SPAN * blocks):
        pick = jnp.int32(0)
        for j in range(1, 4):
            pick = jnp.where(jnp.logical_and(valids[j], places[j] == i), j, pick)
        sel[i] = pick

    def exchange_copy(par, kk, ss):
        mine = (k - kk + REACH) * blocks + s
        theirs = (kk - k + REACH) * blocks + ss
        send = pltpu.make_async_remote_copy(
            src_ref=SEND.at[par, theirs], dst_ref=RECV.at[par, mine],
            send_sem=xs_sem.at[par, theirs], recv_sem=xr_sem.at[par, mine],
            device_id=(ss, kk), device_id_type=MESH,
        )
        recv = pltpu.make_async_remote_copy(
            src_ref=SEND.at[par, theirs], dst_ref=RECV.at[par, theirs],
            send_sem=xs_sem.at[par, theirs], recv_sem=xr_sem.at[par, theirs],
            device_id=(ss, kk), device_id_type=MESH,
        )
        return send, recv

    def each_partner(action):
        def body(kk, carry):
            for ss in range(blocks):
                @pl.when(jnp.logical_not(jnp.logical_and(s == ss, kk == k)))
                def _():
                    action(kk, ss)

            return carry

        lax.fori_loop(lo, hi, body, 0)

    def start_exchange(par, faces):
        F[...] = jnp.concatenate([faces, faces], axis=1).reshape(4, SIDE, 128)
        for i in range(SPAN * blocks):
            SEND[par, i] = F[sel[i]]
        each_partner(lambda kk, ss: exchange_copy(par, kk, ss)[0].start())

    def end_exchange(par):
        each_partner(lambda kk, ss: exchange_copy(par, kk, ss)[1].wait())
        HELD[...] = RECV[par]
        got = []
        for j in range(4):
            face = HELD[places[j]][:, :64]
            got.append(jnp.where(valids[j], face.astype(jnp.float32), 0.0).astype(bf))
        return got

    def result_copy(which, b, ref, src):
        return pltpu.make_async_remote_copy(
            src_ref=src, dst_ref=ref.at[s],
            send_sem=os_sem.at[which, b], recv_sem=or_sem.at[which, s],
            device_id=(b, k), device_id_type=MESH,
        )

    def result_local(which, ref, src):
        return pltpu.make_async_copy(src, ref.at[s], ol_sem.at[which])

    def send_result(which, b, ref, src):
        @pl.when(b != s)
        def _():
            result_copy(which, b, ref, src).start()

        @pl.when(b == s)
        def _():
            result_local(which, ref, src).start()

    def derivative(v):
        sig = sigmoid(v)
        return sig * (1.0 + v * (1.0 - sig))

    def tail_derivatives(b):
        D2[b] = derivative(pre2_s[...]) * NS[b][:, 64:128]
        D3[b] = derivative(pre3_s[...])

    for i, (src, dst) in enumerate(weights):
        pltpu.make_async_copy(src, dst.at[s], wl_sem.at[i]).wait()
    feat_copy.wait()

    def forward(b, carry):
        par = lax.rem(b, 2)

        @pl.when(b != s)
        def _():
            for i in range(len(weights)):
                weight_copy(i, b, b).wait_recv()

        a = acts[b]
        scale = NS[b]
        shift = NT[b]
        pre1 = mm(a, W1[b]) * scale[:, :64] + shift[:, :64]
        sig = sigmoid(pre1)
        h1 = (pre1 * sig).astype(bf)
        start_exchange(par, mm(face_ref[...], h1).astype(bf))
        D1[b] = sig * (1.0 + pre1 * (1.0 - sig)) * scale[:, :64]

        @pl.when(b > 0)
        def _():
            tail_derivatives(b - 1)

        got = end_exchange(par)
        full = jnp.concatenate([got[0], h1, got[1], got[2], got[3]], axis=0)
        moved = mm(shift_ref[...], full).astype(bf)
        cat = jnp.concatenate([moved[:EXT], full[:EXT], moved[EXT:]], axis=1)
        CAT[b] = cat
        pre2 = mm(cat[:PIX], WT[b, :192])
        pre2 += mm(cat[SIDE : SIDE + PIX], WT[b, 192:384])
        pre2 += mm(cat[2 * SIDE :], WT[b, 384:])
        pre2 = pre2 * scale[:, 64:128] + shift[:, 64:128]
        pre2_s[...] = pre2
        h2 = (pre2 * sigmoid(pre2)).astype(bf)
        H2[b] = h2
        pre3 = a.astype(jnp.float32) + mm(h2, W3[b]) * scale[:, 128:] + shift[:, 128:]
        pre3_s[...] = pre3
        acts[b + 1] = (pre3 * sigmoid(pre3)).astype(bf)
        send_result(0, b, out_ref, acts.at[b + 1])
        return carry

    lax.fori_loop(0, blocks, forward, 0)
    tail_derivatives(blocks - 1)
    cot_copy.wait()
    dins[blocks] = cot[...]

    def grad_copy(b):
        return pltpu.make_async_remote_copy(
            src_ref=G.at[b], dst_ref=GR.at[s],
            send_sem=gs_sem.at[b], recv_sem=gr_sem.at[s],
            device_id=(b, k), device_id_type=MESH,
        )

    def backward(step, carry):
        b = blocks - 1 - step
        par = lax.rem(step, 2)
        scale = NS[b]
        d3 = dins[b + 1].astype(jnp.float32) * D3[b]
        DD3[...] = d3
        e3 = (d3 * scale[:, 128:]).astype(bf)
        d2 = (mm_t(e3, W3[b]) * D2[b]).astype(bf)
        p0 = mm_t(d2, WT[b, :192])
        p1 = mm_t(d2, WT[b, 192:384])
        p2 = mm_t(d2, WT[b, 384:])
        zero = jnp.zeros((SIDE, 192), jnp.float32)
        dcat = (
            jnp.concatenate([p0, zero, zero], axis=0)
            + jnp.concatenate([zero, p1, zero], axis=0)
            + jnp.concatenate([zero, zero, p2], axis=0)
        )
        sides = jnp.concatenate([dcat[:, :64], dcat[:, 128:]], axis=0).astype(bf)
        dfull = mm(shift_t_ref[...], sides)
        dmid = (dfull[:EXT] + dcat[:, 64:128]).astype(bf)
        start_exchange(
            par,
            jnp.concatenate([dmid[:SIDE], dmid[SIDE + PIX :], dfull[EXT:].astype(bf)], axis=0),
        )
        taps = jnp.concatenate(
            [t_mm(CAT[b, SIDE * dy : SIDE * dy + PIX], d2) for dy in range(3)], axis=0
        )
        G[b, :288] = jnp.concatenate([taps[:288], taps[288:]], axis=1).astype(bf)
        expand = t_mm(H2[b], e3)
        G[b, 288:352] = expand[:, :128].astype(bf)
        G[b, 352:416] = expand[:, 128:].astype(bf)
        got = end_exchange(par)
        dh1 = dmid[SIDE : SIDE + PIX].astype(jnp.float32) + mm(
            face_t_ref[...], jnp.concatenate(got, axis=0)
        )
        d1 = (dh1 * D1[b]).astype(bf)
        dins[b] = (DD3[...] + mm_t(d1, W1[b])).astype(bf)
        send_result(1, b, din_ref, dins.at[b])
        red = t_mm(acts[b], d1)
        G[b, 416:ROWS] = jnp.concatenate([red[:128], red[128:]], axis=1).astype(bf)
        if owners * chunk > ROWS:
            G[b, ROWS:] = jnp.zeros((owners * chunk - ROWS, 128), bf)

        @pl.when(b != s)
        def _():
            grad_copy(b).start()

        return carry

    lax.fori_loop(0, blocks, backward, 0)

    for ss in range(blocks):
        @pl.when(s != ss)
        def _():
            pltpu.make_async_remote_copy(
                src_ref=G.at[ss], dst_ref=GR.at[ss], send_sem=gs_sem.at[ss],
                recv_sem=gr_sem.at[ss], device_id=(ss, k), device_id_type=MESH,
            ).wait()

    total = G[s].astype(jnp.float32)
    for hop in range(1, blocks):
        total += GR[lax.rem(s + hop, blocks)].astype(jnp.float32)
    G[s] = total.astype(bf)

    def part_send(kk):
        return pltpu.make_async_remote_copy(
            src_ref=G.at[s, pl.ds(pl.multiple_of(kk * chunk, 16), chunk)], dst_ref=P2.at[k],
            send_sem=ps_sem.at[kk], recv_sem=pr_sem.at[k],
            device_id=(s, kk), device_id_type=MESH,
        )

    def part_recv(kk):
        return pltpu.make_async_remote_copy(
            src_ref=P2.at[kk], dst_ref=P2.at[kk], send_sem=ps_sem.at[kk], recv_sem=pr_sem.at[kk],
            device_id=(s, kk), device_id_type=MESH,
        )

    def final_copy(kk, slot):
        return pltpu.make_async_remote_copy(
            src_ref=FIN.at[slot], dst_ref=FIN.at[slot],
            send_sem=fs_sem.at[kk], recv_sem=fr_sem.at[slot],
            device_id=(s, kk), device_id_type=MESH,
        )

    def others(count, action):
        def body(kk, carry):
            @pl.when(kk != k)
            def _():
                action(kk)

            return carry

        lax.fori_loop(0, count, body, 0)

    others(owners, lambda kk: part_send(kk).start())

    @pl.when(k < owners)
    def _():
        P2[k] = G[s, pl.ds(pl.multiple_of(k * chunk, 16), chunk)]
        others(n, lambda kk: part_recv(kk).wait_recv())
        acc = lax.fori_loop(
            0, n, lambda i, acc: acc + P2[i].astype(jnp.float32),
            jnp.zeros((chunk, 128), jnp.float32),
        )
        FIN[k] = acc.astype(bf)
        others(n, lambda kk: final_copy(kk, k).start())

    others(owners, lambda kk: final_copy(kk, kk).wait_recv())
    done = FIN[...].reshape(owners * chunk, 128).astype(jnp.float32)
    gt_ref[0, :288] = done[:288, :64]
    gt_ref[0, 288:] = done[:288, 64:]
    ge_ref[0, :, :128] = done[288:352]
    ge_ref[0, :, 128:] = done[352:416]
    gr_ref[0, :128] = done[416:ROWS, :64]
    gr_ref[0, 128:] = done[416:ROWS, 64:]

    others(owners, lambda kk: part_send(kk).wait_send())

    @pl.when(k < owners)
    def _():
        others(n, lambda kk: final_copy(kk, k).wait_send())

    for ss in range(blocks):
        @pl.when(s != ss)
        def _():
            for i in range(len(weights)):
                weight_copy(i, ss, ss).wait_send()
            for which, ref, held in ((0, out_ref, acts.at[ss + 1]), (1, din_ref, dins.at[ss])):
                pltpu.make_async_remote_copy(
                    src_ref=held, dst_ref=ref.at[ss],
                    send_sem=os_sem.at[which, ss], recv_sem=or_sem.at[which, ss],
                    device_id=(ss, k), device_id_type=MESH,
                ).wait()

    result_local(0, out_ref, acts.at[s + 1]).wait()
    result_local(1, din_ref, dins.at[s]).wait()


def on_device(
    features, out_cotangent, w_reduce, w_taps, w_expand, norm_scale, norm_shift, owner, neighbours
):
    blocks = lax.axis_size("section")
    n = lax.axis_size("tile")
    slots, side, _, chans = features.shape
    bf, f32 = jnp.bfloat16, jnp.float32
    chunk = 16 * max(1, -(-ROWS // (16 * n)))
    owners = -(-ROWS // chunk)
    shift, face = shift_matrices()
    consts = [jnp.asarray(m, bf) for m in (shift, shift.T, face, face.T)]
    vmem = pl.BlockSpec(memory_space=pltpu.VMEM)
    smem = pl.BlockSpec(memory_space=pltpu.SMEM)
    anyw = pl.BlockSpec(memory_space=pl.ANY)
    dma = pltpu.SemaphoreType.DMA
    spots = SPAN * blocks
    results = pl.pallas_call(
        partial(kernel, n, blocks, chunk, owners),
        out_shape=(
            jax.ShapeDtypeStruct((slots, PIX, chans), bf),
            jax.ShapeDtypeStruct((slots, PIX, chans), bf),
            jax.ShapeDtypeStruct((1, 256, 64), f32),
            jax.ShapeDtypeStruct((1, 576, 64), f32),
            jax.ShapeDtypeStruct((1, 64, 256), f32),
        ),
        in_specs=[smem] * 2 + [anyw] * 7 + [vmem] * 4,
        out_specs=[anyw] * 2 + [vmem] * 3,
        scratch_shapes=[
            pltpu.SMEM((spots,), jnp.int32),
            pltpu.VMEM((blocks + 1, PIX, chans), bf),
            pltpu.VMEM((PIX, chans), bf),
            pltpu.VMEM((blocks + 1, PIX, chans), bf),
            pltpu.VMEM((blocks, 256, 64), bf),
            pltpu.VMEM((blocks, 576, 64), bf),
            pltpu.VMEM((blocks, 64, 256), bf),
            pltpu.VMEM((blocks, 1, 384), f32),
            pltpu.VMEM((blocks, 1, 384), f32),
            pltpu.VMEM((blocks, PIX, 64), f32),
            pltpu.VMEM((blocks, PIX, 64), f32),
            pltpu.VMEM((blocks, PIX, chans), f32),
            pltpu.VMEM((PIX, 64), f32),
            pltpu.VMEM((PIX, chans), f32),
            pltpu.VMEM((blocks, EXT, 192), bf),
            pltpu.VMEM((blocks, PIX, 64), bf),
            pltpu.VMEM((PIX, chans), bf),
            pltpu.VMEM((PIX, chans), f32),
            pltpu.VMEM((4, SIDE, 128), bf),
            pltpu.VMEM((2, spots, SIDE, 128), bf),
            pltpu.VMEM((2, spots, SIDE, 128), bf),
            pltpu.VMEM((spots, SIDE, 128), bf),
            pltpu.VMEM((blocks, owners * chunk, 128), bf),
            pltpu.VMEM((blocks, owners * chunk, 128), bf),
            pltpu.VMEM((n, chunk, 128), bf),
            pltpu.VMEM((owners, chunk, 128), bf),
            dma((2,)), dma((5,)), dma((5, blocks)), dma((5, blocks)),
            dma((2, spots)), dma((2, spots)),
            dma((2, blocks)), dma((2, blocks)), dma((2,)),
            dma((blocks,)), dma((blocks,)), dma((owners,)), dma((n,)), dma((n,)), dma((owners,)),
        ],
        compiler_params=pltpu.CompilerParams(
            collective_id=0, has_side_effects=True, vmem_limit_bytes=40 * 1024 * 1024
        ),
        name="residual_blocks",
    )(
        owner, neighbours.reshape(-1),
        features.reshape(slots, PIX, chans), out_cotangent.reshape(slots, PIX, chans),
        w_reduce, w_taps, w_expand, norm_scale, norm_shift, *consts,
    )
    shape = (1, slots, side, side, chans)
    return (results[0].reshape(shape), results[1].reshape(shape)) + tuple(results[2:])


def solution(mesh):
    return jax.shard_map(
        on_device,
        mesh=mesh,
        in_specs=(
            P("tile", None, None, None),
            P("tile", None, None, None),
            P("section", None, None),
            P("section", None, None),
            P("section", None, None),
            P("section", None),
            P("section", None),
            P(),
            P(),
        ),
        out_specs=(
            P("section", "tile", None, None, None),
            P("section", "tile", None, None, None),
            P("section", None, None),
            P("section", None, None),
            P("section", None, None),
        ),
        check_vma=False,
    )
```

```python
from functools import partial

import jax
import jax.numpy as jnp
import numpy as np
from jax import lax
from jax.experimental import pallas as pl
from jax.experimental.pallas import tpu as pltpu
from jax.sharding import PartitionSpec as P

REACH = 3
SPAN = 2 * REACH + 1
MESH = pl.DeviceIdType.MESH
SIDE = 16
PIX = SIDE * SIDE
EXT = PIX + 2 * SIDE
FULL = EXT + 2 * SIDE
ROWS = 544


def shift_matrices():
    left = np.zeros((EXT, FULL), np.float32)
    right = np.zeros((EXT, FULL), np.float32)
    for r in range(EXT):
        y, x = r // SIDE - 1, r % SIDE
        inside = 0 <= y < SIDE
        if x > 0:
            left[r, r - 1] = 1
        elif inside:
            left[r, EXT + y] = 1
        if x < SIDE - 1:
            right[r, r + 1] = 1
        elif inside:
            right[r, EXT + SIDE + y] = 1
    face = np.zeros((4 * SIDE, PIX), np.float32)
    for i in range(SIDE):
        face[i, i] = 1
        face[SIDE + i, PIX - SIDE + i] = 1
        face[2 * SIDE + i, SIDE * i] = 1
        face[3 * SIDE + i, SIDE * i + SIDE - 1] = 1
    return np.concatenate([left, right]), face


def sigmoid(v):
    return 0.5 * jnp.tanh(0.5 * v) + 0.5


def mm(left, right):
    return jnp.dot(left, right, preferred_element_type=jnp.float32)


def mm_t(left, right):
    return lax.dot_general(
        left, right, (((1,), (1,)), ((), ())), preferred_element_type=jnp.float32
    )


def t_mm(left, right):
    return lax.dot_general(
        left, right, (((0,), (0,)), ((), ())), preferred_element_type=jnp.float32
    )


def kernel(
    n, blocks, chunk, owners,
    owner_ref, near_ref, feat_ref, cot_ref, w1_ref, wt_ref, w3_ref, sc_ref, sh_ref,
    shift_in, shift_t_in, face_in, face_t_in,
    out_ref, din_ref, gr_ref, gt_ref, ge_ref,
    sel, shift_ref, shift_t_ref, face_ref, face_t_ref, acts, dins, W1, WT, W3, WC, NS, NT,
    D1, D2, D3, pre2_s, pre3_s, CAT, H2, DD3, F, SEND, RECV, HELD, G, GR, P2, FIN,
    load_sem, const_sem, wl_sem, ws_sem, wr_sem, xs_sem, xr_sem,
    os_sem, or_sem, ol_sem, gs_sem, gr_sem, ps_sem, pr_sem, fs_sem, fr_sem,
):
    s = lax.axis_index("section")
    k = lax.axis_index("tile")
    lo = jnp.maximum(k - REACH, 0)
    hi = jnp.minimum(k + REACH + 1, n)
    bf = jnp.bfloat16

    feat_copy = pltpu.make_async_copy(feat_ref.at[s], acts.at[0], load_sem.at[0])
    cot_copy = pltpu.make_async_copy(cot_ref.at[s], dins.at[blocks], load_sem.at[1])
    const_copies = [
        pltpu.make_async_copy(src, dst, const_sem.at[i])
        for i, (src, dst) in enumerate([
            (face_in, face_ref), (shift_in, shift_ref),
            (shift_t_in, shift_t_ref), (face_t_in, face_t_ref),
        ])
    ]
    feat_copy.start()
    weights = [
        (w1_ref.at[0], W1), (sc_ref, NS), (sh_ref, NT), (wt_ref.at[0], WT), (w3_ref.at[0], W3)
    ]
    for i, (src, dst) in enumerate(weights):
        pltpu.make_async_copy(src, dst.at[s], wl_sem.at[i]).start()
    for copy in const_copies:
        copy.start()
    cot_copy.start()

    barrier = pltpu.get_barrier_semaphore()

    def greet(kk, total):
        near = jnp.logical_and(kk >= lo, kk < hi)
        for ss in range(blocks):
            go = jnp.logical_and(
                jnp.logical_or(near, s == ss), jnp.logical_not(jnp.logical_and(s == ss, kk == k))
            )

            @pl.when(go)
            def _():
                pl.semaphore_signal(barrier, inc=1, device_id=(ss, kk), device_id_type=MESH)

        return total

    lax.fori_loop(0, n, greet, 0)
    slot = k * blocks + s
    tiles = owner_ref.shape[0]
    tile = lax.fori_loop(
        0, tiles, lambda i, acc: jnp.where(owner_ref[i] == slot, i, acc), jnp.int32(0)
    )
    places, valids = [], []
    for j in range(4):
        near = near_ref[tile * 4 + j]
        valid = near >= 0
        where = owner_ref[jnp.where(valid, near, 0)]
        place = (where // blocks - k + REACH) * blocks + where % blocks
        place = jnp.where(valid, place, 0)
        places.append(jnp.clip(place, 0, SPAN * blocks - 1))
        valids.append(valid)
    for i in range(SPAN * blocks):
        pick = jnp.int32(0)
        for j in range(1, 4):
            pick = jnp.where(jnp.logical_and(valids[j], places[j] == i), j, pick)
        sel[i] = pick

    pl.semaphore_wait(barrier, (hi - lo) * (blocks - 1) + n - 1)

    def weight_copy(i, target, slot):
        src, dst = weights[i]
        return pltpu.make_async_remote_copy(
            src_ref=src, dst_ref=dst.at[slot],
            send_sem=ws_sem.at[i, target], recv_sem=wr_sem.at[i, slot],
            device_id=(target, k), device_id_type=MESH,
        )

    def send_weights():
        for i in range(len(weights)):
            for target in range(blocks):
                @pl.when(s != target)
                def _():
                    weight_copy(i, target, s).start()

    @pl.when(s == 0)
    def _():
        send_weights()

    def exchange_copy(par, kk, ss):
        mine = (k - kk + REACH) * blocks + s
        theirs = (kk - k + REACH) * blocks + ss
        send = pltpu.make_async_remote_copy(
            src_ref=SEND.at[par, theirs], dst_ref=RECV.at[par, mine],
            send_sem=xs_sem.at[par, theirs], recv_sem=xr_sem.at[par, mine],
            device_id=(ss, kk), device_id_type=MESH,
        )
        recv = pltpu.make_async_remote_copy(
            src_ref=SEND.at[par, theirs], dst_ref=RECV.at[par, theirs],
            send_sem=xs_sem.at[par, theirs], recv_sem=xr_sem.at[par, theirs],
            device_id=(ss, kk), device_id_type=MESH,
        )
        return send, recv

    def each_partner(action):
        def body(kk, carry):
            for ss in range(blocks):
                @pl.when(jnp.logical_not(jnp.logical_and(s == ss, kk == k)))
                def _():
                    action(kk, ss)

            return carry

        lax.fori_loop(lo, hi, body, 0)

    def start_exchange(par, faces):
        F[...] = jnp.concatenate([faces, faces], axis=1).reshape(4, SIDE, 128)
        for i in range(SPAN * blocks):
            SEND[par, i] = F[sel[i]]
        each_partner(lambda kk, ss: exchange_copy(par, kk, ss)[0].start())

    def end_exchange(par):
        each_partner(lambda kk, ss: exchange_copy(par, kk, ss)[1].wait())
        HELD[...] = RECV[par]
        got = []
        for j in range(4):
            face = HELD[places[j]][:, :64]
            got.append(jnp.where(valids[j], face.astype(jnp.float32), 0.0).astype(bf))
        return got

    def result_copy(which, b, ref, src):
        return pltpu.make_async_remote_copy(
            src_ref=src, dst_ref=ref.at[s],
            send_sem=os_sem.at[which, b], recv_sem=or_sem.at[which, s],
            device_id=(b, k), device_id_type=MESH,
        )

    def result_local(which, ref, src):
        return pltpu.make_async_copy(src, ref.at[s], ol_sem.at[which])

    def send_result(which, b, ref, src):
        @pl.when(b != s)
        def _():
            result_copy(which, b, ref, src).start()

        @pl.when(b == s)
        def _():
            result_local(which, ref, src).start()

    def derivative(v):
        sig = sigmoid(v)
        return sig * (1.0 + v * (1.0 - sig))

    def tail_derivatives(b):
        D2[b] = derivative(pre2_s[...]) * NS[b][:, 64:128]
        D3[b] = derivative(pre3_s[...])

    for i, (src, dst) in enumerate(weights):
        pltpu.make_async_copy(src, dst.at[s], wl_sem.at[i]).wait()
    feat_copy.wait()
    for copy in const_copies:
        copy.wait()

    def forward(b, carry):
        par = lax.rem(b, 2)

        @pl.when(b != s)
        def _():
            for i in range(len(weights)):
                weight_copy(i, b, b).wait_recv()

        a = acts[b]
        scale = NS[b]
        shift = NT[b]
        pre1 = mm_t(a, W1[b]) * scale[:, :64] + shift[:, :64]
        sig = sigmoid(pre1)
        h1 = (pre1 * sig).astype(bf)
        start_exchange(par, mm(face_ref[...], h1).astype(bf))

        @pl.when(b > 0)
        def _():
            send_result(0, b - 1, out_ref, acts.at[b])
            tail_derivatives(b - 1)

        @pl.when(jnp.logical_and(b == 0, s != 0))
        def _():
            send_weights()

        D1[b] = sig * (1.0 + pre1 * (1.0 - sig)) * scale[:, :64]
        taps = WT[b]
        WC[b] = jnp.concatenate([taps[:, :192], taps[:, 192:384], taps[:, 384:]], axis=0)

        got = end_exchange(par)
        full = jnp.concatenate([got[0], h1, got[1], got[2], got[3]], axis=0)
        moved = mm(shift_ref[...], full).astype(bf)
        cat = jnp.concatenate([moved[:EXT], full[:EXT], moved[EXT:]], axis=1)
        CAT[b] = cat
        rows = mm_t(cat, WC[b])
        pre2 = (
            rows[:PIX, :64] + rows[SIDE : SIDE + PIX, 64:128] + rows[2 * SIDE :, 128:]
        )
        pre2 = pre2 * scale[:, 64:128] + shift[:, 64:128]
        pre2_s[...] = pre2
        h2 = (pre2 * sigmoid(pre2)).astype(bf)
        H2[b] = h2
        pre3 = a.astype(jnp.float32) + mm(h2, W3[b]) * scale[:, 128:] + shift[:, 128:]
        pre3_s[...] = pre3
        acts[b + 1] = (pre3 * sigmoid(pre3)).astype(bf)
        return carry

    lax.fori_loop(0, blocks, forward, 0)
    tail_derivatives(blocks - 1)
    cot_copy.wait()

    def grad_copy(part, b, slot):
        rows = pl.ds(0, 416) if part == 0 else pl.ds(416, ROWS - 416)
        return pltpu.make_async_remote_copy(
            src_ref=G.at[b, rows], dst_ref=GR.at[slot, rows],
            send_sem=gs_sem.at[part, b], recv_sem=gr_sem.at[part, slot],
            device_id=(b, k), device_id_type=MESH,
        )

    def send_grads(part, b):
        @pl.when(b != s)
        def _():
            grad_copy(part, b, s).start()

    def backward(step, carry):
        b = blocks - 1 - step
        par = lax.rem(step, 2)
        scale = NS[b]
        d3 = dins[b + 1].astype(jnp.float32) * D3[b]
        DD3[...] = d3
        e3 = (d3 * scale[:, 128:]).astype(bf)
        d2 = (mm_t(e3, W3[b]) * D2[b]).astype(bf)
        zero = jnp.zeros((SIDE, 64), bf)
        d2cat = jnp.concatenate(
            [
                jnp.concatenate([d2, zero, zero], axis=0),
                jnp.concatenate([zero, d2, zero], axis=0),
                jnp.concatenate([zero, zero, d2], axis=0),
            ],
            axis=1,
        )
        dcat = mm(d2cat, WC[b])
        sides = jnp.concatenate([dcat[:, :64], dcat[:, 128:]], axis=0).astype(bf)
        dfull = mm(shift_t_ref[...], sides)
        dmid = (dfull[:EXT] + dcat[:, 64:128]).astype(bf)
        start_exchange(
            par,
            jnp.concatenate([dmid[:SIDE], dmid[SIDE + PIX :], dfull[EXT:].astype(bf)], axis=0),
        )
        taps = t_mm(d2cat, CAT[b]).astype(bf)
        G[b, :192] = taps[:, :128]
        G[b, 192:288] = jnp.concatenate([taps[:96, 128:], taps[96:, 128:]], axis=1)
        expand = t_mm(H2[b], e3).astype(bf)
        G[b, 288:352] = expand[:, :128]
        G[b, 352:416] = expand[:, 128:]
        send_grads(0, b)

        @pl.when(step == 0)
        def _():
            send_result(0, blocks - 1, out_ref, acts.at[blocks])

        @pl.when(step > 0)
        def _():
            send_result(1, b + 1, din_ref, dins.at[b + 1])

        got = end_exchange(par)
        dh1 = dmid[SIDE : SIDE + PIX].astype(jnp.float32) + mm(
            face_t_ref[...], jnp.concatenate(got, axis=0)
        )
        d1 = (dh1 * D1[b]).astype(bf)
        red = t_mm(d1, acts[b]).astype(bf)
        G[b, 416:480] = red[:, :128]
        G[b, 480:ROWS] = red[:, 128:]
        if owners * chunk > ROWS:
            G[b, ROWS:] = jnp.zeros((owners * chunk - ROWS, 128), bf)
        send_grads(1, b)
        dins[b] = (DD3[...] + mm(d1, W1[b])).astype(bf)
        return carry

    lax.fori_loop(0, blocks, backward, 0)
    send_result(1, 0, din_ref, dins.at[0])

    for ss in range(blocks):
        @pl.when(s != ss)
        def _():
            grad_copy(0, ss, ss).wait()
            grad_copy(1, ss, ss).wait()

    total = G[s, :ROWS].astype(jnp.float32)
    for hop in range(1, blocks):
        total += GR[lax.rem(s + hop, blocks), :ROWS].astype(jnp.float32)
    G[s, :ROWS] = total.astype(bf)

    def part_send(kk):
        return pltpu.make_async_remote_copy(
            src_ref=G.at[s, pl.ds(pl.multiple_of(kk * chunk, 16), chunk)], dst_ref=P2.at[k],
            send_sem=ps_sem.at[kk], recv_sem=pr_sem.at[k],
            device_id=(s, kk), device_id_type=MESH,
        )

    def part_recv(kk):
        return pltpu.make_async_remote_copy(
            src_ref=P2.at[kk], dst_ref=P2.at[kk], send_sem=ps_sem.at[kk], recv_sem=pr_sem.at[kk],
            device_id=(s, kk), device_id_type=MESH,
        )

    def final_copy(kk, slot):
        return pltpu.make_async_remote_copy(
            src_ref=FIN.at[slot], dst_ref=FIN.at[slot],
            send_sem=fs_sem.at[kk], recv_sem=fr_sem.at[slot],
            device_id=(s, kk), device_id_type=MESH,
        )

    def others(count, action):
        def body(kk, carry):
            @pl.when(kk != k)
            def _():
                action(kk)

            return carry

        lax.fori_loop(0, count, body, 0)

    others(owners, lambda kk: part_send(kk).start())

    @pl.when(k < owners)
    def _():
        P2[k] = G[s, pl.ds(pl.multiple_of(k * chunk, 16), chunk)]
        others(n, lambda kk: part_recv(kk).wait_recv())
        acc = lax.fori_loop(
            0, n, lambda i, acc: acc + P2[i].astype(jnp.float32),
            jnp.zeros((chunk, 128), jnp.float32),
        )
        FIN[k] = acc.astype(bf)
        others(n, lambda kk: final_copy(kk, k).start())

    others(owners, lambda kk: final_copy(kk, kk).wait_recv())
    done = FIN[...].reshape(owners * chunk, 128).astype(jnp.float32)
    right = jnp.concatenate([done[192:288, :64], done[192:288, 64:]], axis=0)
    for dy in range(3):
        span = slice(64 * dy, 64 * dy + 64)
        gt_ref[0, :, 192 * dy : 192 * dy + 192] = jnp.concatenate(
            [done[span], right[span]], axis=1
        )
    ge_ref[0, :, :128] = done[288:352]
    ge_ref[0, :, 128:] = done[352:416]
    gr_ref[0, :, :128] = done[416:480]
    gr_ref[0, :, 128:] = done[480:ROWS]

    others(owners, lambda kk: part_send(kk).wait_send())

    @pl.when(k < owners)
    def _():
        others(n, lambda kk: final_copy(kk, k).wait_send())

    for ss in range(blocks):
        @pl.when(s != ss)
        def _():
            for i in range(len(weights)):
                weight_copy(i, ss, ss).wait_send()
            for which, ref, held in ((0, out_ref, acts.at[ss + 1]), (1, din_ref, dins.at[ss])):
                pltpu.make_async_remote_copy(
                    src_ref=held, dst_ref=ref.at[ss],
                    send_sem=os_sem.at[which, ss], recv_sem=or_sem.at[which, ss],
                    device_id=(ss, k), device_id_type=MESH,
                ).wait()

    result_local(0, out_ref, acts.at[s + 1]).wait()
    result_local(1, din_ref, dins.at[s]).wait()


def on_device(
    features, out_cotangent, w_reduce, w_taps, w_expand, norm_scale, norm_shift, owner, neighbours
):
    blocks = lax.axis_size("section")
    n = lax.axis_size("tile")
    slots, side, _, chans = features.shape
    bf, f32 = jnp.bfloat16, jnp.float32
    chunk = 16 * max(1, -(-ROWS // (16 * n)))
    owners = -(-ROWS // chunk)
    shift, face = shift_matrices()
    consts = [jnp.asarray(m, bf) for m in (shift, shift.T, face, face.T)]
    vmem = pl.BlockSpec(memory_space=pltpu.VMEM)
    smem = pl.BlockSpec(memory_space=pltpu.SMEM)
    anyw = pl.BlockSpec(memory_space=pl.ANY)
    dma = pltpu.SemaphoreType.DMA
    spots = SPAN * blocks
    results = pl.pallas_call(
        partial(kernel, n, blocks, chunk, owners),
        out_shape=(
            jax.ShapeDtypeStruct((slots, PIX, chans), bf),
            jax.ShapeDtypeStruct((slots, PIX, chans), bf),
            jax.ShapeDtypeStruct((1, 64, 256), f32),
            jax.ShapeDtypeStruct((1, 64, 576), f32),
            jax.ShapeDtypeStruct((1, 64, 256), f32),
        ),
        in_specs=[smem] * 2 + [anyw] * 11,
        out_specs=[anyw] * 2 + [vmem] * 3,
        scratch_shapes=[
            pltpu.SMEM((spots,), jnp.int32),
            *[pltpu.VMEM(m.shape, bf) for m in consts],
            pltpu.VMEM((blocks + 1, PIX, chans), bf),
            pltpu.VMEM((blocks + 1, PIX, chans), bf),
            pltpu.VMEM((blocks, 64, 256), bf),
            pltpu.VMEM((blocks, 64, 576), bf),
            pltpu.VMEM((blocks, 64, 256), bf),
            pltpu.VMEM((blocks, 192, 192), bf),
            pltpu.VMEM((blocks, 1, 384), f32),
            pltpu.VMEM((blocks, 1, 384), f32),
            pltpu.VMEM((blocks, PIX, 64), f32),
            pltpu.VMEM((blocks, PIX, 64), f32),
            pltpu.VMEM((blocks, PIX, chans), f32),
            pltpu.VMEM((PIX, 64), f32),
            pltpu.VMEM((PIX, chans), f32),
            pltpu.VMEM((blocks, EXT, 192), bf),
            pltpu.VMEM((blocks, PIX, 64), bf),
            pltpu.VMEM((PIX, chans), f32),
            pltpu.VMEM((4, SIDE, 128), bf),
            pltpu.VMEM((2, spots, SIDE, 128), bf),
            pltpu.VMEM((2, spots, SIDE, 128), bf),
            pltpu.VMEM((spots, SIDE, 128), bf),
            pltpu.VMEM((blocks, owners * chunk, 128), bf),
            pltpu.VMEM((blocks, owners * chunk, 128), bf),
            pltpu.VMEM((n, chunk, 128), bf),
            pltpu.VMEM((owners, chunk, 128), bf),
            dma((2,)), dma((4,)), dma((5,)), dma((5, blocks)), dma((5, blocks)),
            dma((2, spots)), dma((2, spots)),
            dma((2, blocks)), dma((2, blocks)), dma((2,)),
            dma((2, blocks)), dma((2, blocks)), dma((owners,)), dma((n,)), dma((n,)), dma((owners,)),
        ],
        compiler_params=pltpu.CompilerParams(
            collective_id=0, has_side_effects=True, vmem_limit_bytes=48 * 1024 * 1024
        ),
        name="residual_blocks",
    )(
        owner, neighbours.reshape(-1),
        features.reshape(slots, PIX, chans), out_cotangent.reshape(slots, PIX, chans),
        jnp.swapaxes(w_reduce, 1, 2), jnp.swapaxes(w_taps, 1, 2), w_expand, norm_scale, norm_shift,
        *consts,
    )
    shape = (1, slots, side, side, chans)
    return (
        results[0].reshape(shape), results[1].reshape(shape),
        jnp.swapaxes(results[2], 1, 2), jnp.swapaxes(results[3], 1, 2), results[4],
    )


def solution(mesh):
    return jax.shard_map(
        on_device,
        mesh=mesh,
        in_specs=(
            P("tile", None, None, None),
            P("tile", None, None, None),
            P("section", None, None),
            P("section", None, None),
            P("section", None, None),
            P("section", None),
            P("section", None),
            P(),
            P(),
        ),
        out_specs=(
            P("section", "tile", None, None, None),
            P("section", "tile", None, None, None),
            P("section", None, None),
            P("section", None, None),
            P("section", None, None),
        ),
        check_vma=False,
    )
```

```python
from functools import partial

import jax
import jax.numpy as jnp
import numpy as np
from jax import lax
from jax.experimental import pallas as pl
from jax.experimental.pallas import tpu as pltpu
from jax.sharding import PartitionSpec as P

REACH = 3
SPAN = 2 * REACH + 1
MESH = pl.DeviceIdType.MESH
SIDE = 16
PIX = SIDE * SIDE
EXT = PIX + 2 * SIDE
FULL = EXT + 2 * SIDE
ROWS = 544


def shift_matrices():
    left = np.zeros((EXT, FULL), np.float32)
    right = np.zeros((EXT, FULL), np.float32)
    for r in range(EXT):
        y, x = r // SIDE - 1, r % SIDE
        inside = 0 <= y < SIDE
        if x > 0:
            left[r, r - 1] = 1
        elif inside:
            left[r, EXT + y] = 1
        if x < SIDE - 1:
            right[r, r + 1] = 1
        elif inside:
            right[r, EXT + SIDE + y] = 1
    face = np.zeros((4 * SIDE, PIX), np.float32)
    for i in range(SIDE):
        face[i, i] = 1
        face[SIDE + i, PIX - SIDE + i] = 1
        face[2 * SIDE + i, SIDE * i] = 1
        face[3 * SIDE + i, SIDE * i + SIDE - 1] = 1
    return np.concatenate([left, right]), face


def sigmoid(v):
    return 0.5 * jnp.tanh(0.5 * v) + 0.5


def mm(left, right):
    return jnp.dot(left, right, preferred_element_type=jnp.float32)


def mm_t(left, right):
    return lax.dot_general(
        left, right, (((1,), (1,)), ((), ())), preferred_element_type=jnp.float32
    )


def t_mm(left, right):
    return lax.dot_general(
        left, right, (((0,), (0,)), ((), ())), preferred_element_type=jnp.float32
    )


def kernel(
    n, blocks, chunk, owners,
    owner_ref, near_ref, feat_ref, cot_ref, w1_ref, wt_ref, w3_ref, sc_ref, sh_ref,
    shift_in, shift_t_in, face_in, face_t_in,
    out_ref, din_ref, gr_ref, gt_ref, ge_ref,
    sel, shift_ref, shift_t_ref, face_ref, face_t_ref, acts, dins, W1, WT, W3, WC, NS, NT,
    D1, D2, D3, pre2_s, pre3_s, CAT, H2, DD3, F, SEND, RECV, HELD, G, GR, P2, FIN,
    load_sem, const_sem, wl_sem, ws_sem, wr_sem, xs_sem, xr_sem,
    os_sem, or_sem, ol_sem, gs_sem, gr_sem, ps_sem, pr_sem, fs_sem, fr_sem,
):
    s = lax.axis_index("section")
    k = lax.axis_index("tile")
    lo = jnp.maximum(k - REACH, 0)
    hi = jnp.minimum(k + REACH + 1, n)
    bf = jnp.bfloat16

    feat_copy = pltpu.make_async_copy(feat_ref.at[s], acts.at[0], load_sem.at[0])
    cot_copy = pltpu.make_async_copy(cot_ref.at[s], dins.at[blocks], load_sem.at[1])
    const_copies = [
        pltpu.make_async_copy(src, dst, const_sem.at[i])
        for i, (src, dst) in enumerate([
            (face_in, face_ref), (shift_in, shift_ref),
            (shift_t_in, shift_t_ref), (face_t_in, face_t_ref),
        ])
    ]
    feat_copy.start()
    weights = [
        (w1_ref.at[0], W1), (sc_ref, NS), (sh_ref, NT), (wt_ref.at[0], WT), (w3_ref.at[0], W3)
    ]
    for i, (src, dst) in enumerate(weights):
        pltpu.make_async_copy(src, dst.at[s], wl_sem.at[i]).start()
    for copy in const_copies:
        copy.start()
    cot_copy.start()

    barrier = pltpu.get_barrier_semaphore()

    def greet(kk, total):
        near = jnp.logical_and(kk >= lo, kk < hi)
        for ss in range(blocks):
            go = jnp.logical_and(
                jnp.logical_or(near, s == ss), jnp.logical_not(jnp.logical_and(s == ss, kk == k))
            )

            @pl.when(go)
            def _():
                pl.semaphore_signal(barrier, inc=1, device_id=(ss, kk), device_id_type=MESH)

        return total

    lax.fori_loop(0, n, greet, 0)
    slot = k * blocks + s
    tiles = owner_ref.shape[0]
    tile = lax.fori_loop(
        0, tiles, lambda i, acc: jnp.where(owner_ref[i] == slot, i, acc), jnp.int32(0)
    )
    places, valids = [], []
    for j in range(4):
        near = near_ref[j, tile]
        valid = near >= 0
        where = owner_ref[jnp.where(valid, near, 0)]
        hop = lax.rem(where % blocks - s + blocks, blocks)
        place = (where // blocks - k + REACH) * blocks + hop
        place = jnp.where(valid, place, 0)
        places.append(jnp.clip(place, 0, SPAN * blocks - 1))
        valids.append(valid)
    for i in range(SPAN * blocks):
        pick = jnp.int32(0)
        for j in range(1, 4):
            pick = jnp.where(jnp.logical_and(valids[j], places[j] == i), j, pick)
        sel[i] = pick

    pl.semaphore_wait(barrier, (hi - lo) * (blocks - 1) + n - 1)

    def weight_copy(i, target, slot):
        src, dst = weights[i]
        return pltpu.make_async_remote_copy(
            src_ref=src, dst_ref=dst.at[slot],
            send_sem=ws_sem.at[i, target], recv_sem=wr_sem.at[i, slot],
            device_id=(target, k), device_id_type=MESH,
        )

    def send_weights():
        for i in range(len(weights)):
            for target in range(blocks):
                @pl.when(s != target)
                def _():
                    weight_copy(i, target, s).start()

    @pl.when(s == 0)
    def _():
        send_weights()

    def partners():
        for far in sorted(range(-REACH, REACH + 1), key=lambda o: -abs(o)):
            yield far, [hop for hop in range(blocks) if far or hop]

    def exchange_copy(par, far, hop):
        theirs = (far + REACH) * blocks + hop
        mine = (REACH - far) * blocks + (blocks - hop) % blocks
        return pltpu.make_async_remote_copy(
            src_ref=SEND.at[par, theirs], dst_ref=RECV.at[par, mine],
            send_sem=xs_sem.at[par, theirs], recv_sem=xr_sem.at[par, mine],
            device_id=(lax.rem(s + hop, blocks), k + far), device_id_type=MESH,
        )

    def each_partner(action):
        for far, hops in partners():
            def body():
                for hop in hops:
                    action(far, hop)

            if far:
                pl.when(jnp.logical_and(k + far >= 0, k + far < n))(body)
            else:
                body()

    def sent(par):
        each_partner(lambda far, hop: exchange_copy(par, far, hop).wait_send())

    def start_exchange(par, faces):
        F[...] = jnp.concatenate([faces, faces], axis=1).reshape(4, SIDE, 128)
        for i in range(SPAN * blocks):
            SEND[par, i] = F[sel[i]]
        each_partner(lambda far, hop: exchange_copy(par, far, hop).start())

    def end_exchange(par):
        each_partner(lambda far, hop: exchange_copy(par, -far, -hop % blocks).wait_recv())
        HELD[...] = RECV[par]
        got = []
        for j in range(4):
            face = HELD[places[j]][:, :64]
            got.append(jnp.where(valids[j], face.astype(jnp.float32), 0.0).astype(bf))
        return got

    def result_copy(which, b, ref, src):
        return pltpu.make_async_remote_copy(
            src_ref=src, dst_ref=ref.at[s],
            send_sem=os_sem.at[which, b], recv_sem=or_sem.at[which, s],
            device_id=(b, k), device_id_type=MESH,
        )

    def result_local(which, ref, src):
        return pltpu.make_async_copy(src, ref.at[s], ol_sem.at[which])

    def send_result(which, b, ref, src):
        @pl.when(b != s)
        def _():
            result_copy(which, b, ref, src).start()

        @pl.when(b == s)
        def _():
            result_local(which, ref, src).start()

    def derivative(v):
        sig = sigmoid(v)
        return sig * (1.0 + v * (1.0 - sig))

    def tail_derivatives(b):
        D2[b] = derivative(pre2_s[...]) * NS[b][:, 64:128]
        D3[b] = derivative(pre3_s[...])

    for i, (src, dst) in enumerate(weights):
        pltpu.make_async_copy(src, dst.at[s], wl_sem.at[i]).wait()
    feat_copy.wait()
    for copy in const_copies:
        copy.wait()

    def forward(b, carry):
        par = lax.rem(b, 2)

        @pl.when(b != s)
        def _():
            for i in range(len(weights)):
                weight_copy(i, b, b).wait_recv()

        a = acts[b]
        scale = NS[b]
        shift = NT[b]
        pre1 = mm_t(a, W1[b]) * scale[:, :64] + shift[:, :64]
        sig = sigmoid(pre1)
        h1 = (pre1 * sig).astype(bf)
        start_exchange(par, mm(face_ref[...], h1).astype(bf))

        @pl.when(b > 0)
        def _():
            sent(1 - par)
            send_result(0, b - 1, out_ref, acts.at[b])
            tail_derivatives(b - 1)

        @pl.when(jnp.logical_and(b == 0, s != 0))
        def _():
            send_weights()

        D1[b] = sig * (1.0 + pre1 * (1.0 - sig)) * scale[:, :64]
        taps = WT[b]
        WC[b] = jnp.concatenate([taps[:, :192], taps[:, 192:384], taps[:, 384:]], axis=0)

        got = end_exchange(par)
        full = jnp.concatenate([got[0], h1, got[1], got[2], got[3]], axis=0)
        moved = mm(shift_ref[...], full).astype(bf)
        cat = jnp.concatenate([moved[:EXT], full[:EXT], moved[EXT:]], axis=1)
        CAT[b] = cat
        rows = mm_t(cat, WC[b])
        pre2 = (
            rows[:PIX, :64] + rows[SIDE : SIDE + PIX, 64:128] + rows[2 * SIDE :, 128:]
        )
        pre2 = pre2 * scale[:, 64:128] + shift[:, 64:128]
        pre2_s[...] = pre2
        h2 = (pre2 * sigmoid(pre2)).astype(bf)
        H2[b] = h2
        pre3 = a.astype(jnp.float32) + mm(h2, W3[b]) * scale[:, 128:] + shift[:, 128:]
        pre3_s[...] = pre3
        acts[b + 1] = (pre3 * sigmoid(pre3)).astype(bf)
        return carry

    lax.fori_loop(0, blocks, forward, 0)
    tail_derivatives(blocks - 1)
    cot_copy.wait()

    def grad_copy(part, b, slot):
        rows = pl.ds(0, 416) if part == 0 else pl.ds(416, ROWS - 416)
        return pltpu.make_async_remote_copy(
            src_ref=G.at[b, rows], dst_ref=GR.at[slot, rows],
            send_sem=gs_sem.at[part, b], recv_sem=gr_sem.at[part, slot],
            device_id=(b, k), device_id_type=MESH,
        )

    def send_grads(part, b):
        @pl.when(b != s)
        def _():
            grad_copy(part, b, s).start()

    def backward(step, carry):
        b = blocks - 1 - step
        par = lax.rem(step + blocks, 2)
        scale = NS[b]
        d3 = dins[b + 1].astype(jnp.float32) * D3[b]
        DD3[...] = d3
        e3 = (d3 * scale[:, 128:]).astype(bf)
        d2 = (mm_t(e3, W3[b]) * D2[b]).astype(bf)
        zero = jnp.zeros((SIDE, 64), bf)
        d2cat = jnp.concatenate(
            [
                jnp.concatenate([d2, zero, zero], axis=0),
                jnp.concatenate([zero, d2, zero], axis=0),
                jnp.concatenate([zero, zero, d2], axis=0),
            ],
            axis=1,
        )
        dcat = mm(d2cat, WC[b])
        sides = jnp.concatenate([dcat[:, :64], dcat[:, 128:]], axis=0).astype(bf)
        dfull = mm(shift_t_ref[...], sides)
        dmid = (dfull[:EXT] + dcat[:, 64:128]).astype(bf)
        start_exchange(
            par,
            jnp.concatenate([dmid[:SIDE], dmid[SIDE + PIX :], dfull[EXT:].astype(bf)], axis=0),
        )
        taps = t_mm(d2cat, CAT[b]).astype(bf)
        G[b, :192] = taps[:, :128]
        G[b, 192:288] = jnp.concatenate([taps[:96, 128:], taps[96:, 128:]], axis=1)
        expand = t_mm(H2[b], e3).astype(bf)
        G[b, 288:352] = expand[:, :128]
        G[b, 352:416] = expand[:, 128:]
        send_grads(0, b)
        sent(1 - par)

        @pl.when(step == 0)
        def _():
            send_result(0, blocks - 1, out_ref, acts.at[blocks])

        @pl.when(step > 0)
        def _():
            send_result(1, b + 1, din_ref, dins.at[b + 1])

        got = end_exchange(par)
        dh1 = dmid[SIDE : SIDE + PIX].astype(jnp.float32) + mm(
            face_t_ref[...], jnp.concatenate(got, axis=0)
        )
        d1 = (dh1 * D1[b]).astype(bf)
        red = t_mm(d1, acts[b]).astype(bf)
        G[b, 416:480] = red[:, :128]
        G[b, 480:ROWS] = red[:, 128:]
        if owners * chunk > ROWS:
            G[b, ROWS:] = jnp.zeros((owners * chunk - ROWS, 128), bf)
        send_grads(1, b)
        dins[b] = (DD3[...] + mm(d1, W1[b])).astype(bf)
        return carry

    lax.fori_loop(0, blocks, backward, 0)
    send_result(1, 0, din_ref, dins.at[0])
    sent((2 * blocks - 1) % 2)

    for ss in range(blocks):
        @pl.when(s != ss)
        def _():
            grad_copy(0, ss, ss).wait()
            grad_copy(1, ss, ss).wait()

    total = G[s, :ROWS].astype(jnp.float32)
    for hop in range(1, blocks):
        total += GR[lax.rem(s + hop, blocks), :ROWS].astype(jnp.float32)
    G[s, :ROWS] = total.astype(bf)

    def part_send(kk):
        return pltpu.make_async_remote_copy(
            src_ref=G.at[s, pl.ds(pl.multiple_of(kk * chunk, 16), chunk)], dst_ref=P2.at[k],
            send_sem=ps_sem.at[kk], recv_sem=pr_sem.at[k],
            device_id=(s, kk), device_id_type=MESH,
        )

    def part_recv(kk):
        return pltpu.make_async_remote_copy(
            src_ref=P2.at[kk], dst_ref=P2.at[kk], send_sem=ps_sem.at[kk], recv_sem=pr_sem.at[kk],
            device_id=(s, kk), device_id_type=MESH,
        )

    def final_copy(kk, slot):
        return pltpu.make_async_remote_copy(
            src_ref=FIN.at[slot], dst_ref=FIN.at[slot],
            send_sem=fs_sem.at[kk], recv_sem=fr_sem.at[slot],
            device_id=(s, kk), device_id_type=MESH,
        )

    def others(count, action):
        def body(kk, carry):
            @pl.when(kk != k)
            def _():
                action(kk)

            return carry

        lax.fori_loop(0, count, body, 0)

    others(owners, lambda kk: part_send(kk).start())

    @pl.when(k < owners)
    def _():
        P2[k] = G[s, pl.ds(pl.multiple_of(k * chunk, 16), chunk)]
        others(n, lambda kk: part_recv(kk).wait_recv())
        acc = lax.fori_loop(
            0, n, lambda i, acc: acc + P2[i].astype(jnp.float32),
            jnp.zeros((chunk, 128), jnp.float32),
        )
        FIN[k] = acc.astype(bf)
        others(n, lambda kk: final_copy(kk, k).start())

    others(owners, lambda kk: final_copy(kk, kk).wait_recv())
    done = FIN[...].reshape(owners * chunk, 128).astype(jnp.float32)
    right = jnp.concatenate([done[192:288, :64], done[192:288, 64:]], axis=0)
    for dy in range(3):
        span = slice(64 * dy, 64 * dy + 64)
        gt_ref[0, :, 192 * dy : 192 * dy + 192] = jnp.concatenate(
            [done[span], right[span]], axis=1
        )
    ge_ref[0, :, :128] = done[288:352]
    ge_ref[0, :, 128:] = done[352:416]
    gr_ref[0, :, :128] = done[416:480]
    gr_ref[0, :, 128:] = done[480:ROWS]

    others(owners, lambda kk: part_send(kk).wait_send())

    @pl.when(k < owners)
    def _():
        others(n, lambda kk: final_copy(kk, k).wait_send())

    for ss in range(blocks):
        @pl.when(s != ss)
        def _():
            for i in range(len(weights)):
                weight_copy(i, ss, ss).wait_send()
            for which, ref, held in ((0, out_ref, acts.at[ss + 1]), (1, din_ref, dins.at[ss])):
                pltpu.make_async_remote_copy(
                    src_ref=held, dst_ref=ref.at[ss],
                    send_sem=os_sem.at[which, ss], recv_sem=or_sem.at[which, ss],
                    device_id=(ss, k), device_id_type=MESH,
                ).wait()

    result_local(0, out_ref, acts.at[s + 1]).wait()
    result_local(1, din_ref, dins.at[s]).wait()


def on_device(
    features, out_cotangent, w_reduce, w_taps, w_expand, norm_scale, norm_shift, owner, neighbours
):
    blocks = lax.axis_size("section")
    n = lax.axis_size("tile")
    slots, side, _, chans = features.shape
    bf, f32 = jnp.bfloat16, jnp.float32
    chunk = 16 * max(1, -(-ROWS // (16 * n)))
    owners = -(-ROWS // chunk)
    shift, face = shift_matrices()
    consts = [jnp.asarray(m, bf) for m in (shift, shift.T, face, face.T)]
    vmem = pl.BlockSpec(memory_space=pltpu.VMEM)
    smem = pl.BlockSpec(memory_space=pltpu.SMEM)
    anyw = pl.BlockSpec(memory_space=pl.ANY)
    hbm = pl.BlockSpec(memory_space=pltpu.HBM)
    dma = pltpu.SemaphoreType.DMA
    spots = SPAN * blocks
    results = pl.pallas_call(
        partial(kernel, n, blocks, chunk, owners),
        out_shape=(
            jax.ShapeDtypeStruct((slots, PIX, chans), bf),
            jax.ShapeDtypeStruct((slots, PIX, chans), bf),
            jax.ShapeDtypeStruct((1, 64, 256), f32),
            jax.ShapeDtypeStruct((1, 64, 576), f32),
            jax.ShapeDtypeStruct((1, 64, 256), f32),
        ),
        in_specs=[smem] * 2 + [hbm] * 11,
        out_specs=[anyw] * 2 + [vmem] * 3,
        scratch_shapes=[
            pltpu.SMEM((spots,), jnp.int32),
            *[pltpu.VMEM(m.shape, bf) for m in consts],
            pltpu.VMEM((blocks + 1, PIX, chans), bf),
            pltpu.VMEM((blocks + 1, PIX, chans), bf),
            pltpu.VMEM((blocks, 64, 256), bf),
            pltpu.VMEM((blocks, 64, 576), bf),
            pltpu.VMEM((blocks, 64, 256), bf),
            pltpu.VMEM((blocks, 192, 192), bf),
            pltpu.VMEM((blocks, 1, 384), f32),
            pltpu.VMEM((blocks, 1, 384), f32),
            pltpu.VMEM((blocks, PIX, 64), f32),
            pltpu.VMEM((blocks, PIX, 64), f32),
            pltpu.VMEM((blocks, PIX, chans), f32),
            pltpu.VMEM((PIX, 64), f32),
            pltpu.VMEM((PIX, chans), f32),
            pltpu.VMEM((blocks, EXT, 192), bf),
            pltpu.VMEM((blocks, PIX, 64), bf),
            pltpu.VMEM((PIX, chans), f32),
            pltpu.VMEM((4, SIDE, 128), bf),
            pltpu.VMEM((2, spots, SIDE, 128), bf),
            pltpu.VMEM((2, spots, SIDE, 128), bf),
            pltpu.VMEM((spots, SIDE, 128), bf),
            pltpu.VMEM((blocks, owners * chunk, 128), bf),
            pltpu.VMEM((blocks, owners * chunk, 128), bf),
            pltpu.VMEM((n, chunk, 128), bf),
            pltpu.VMEM((owners, chunk, 128), bf),
            dma((2,)), dma((4,)), dma((5,)), dma((5, blocks)), dma((5, blocks)),
            dma((2, spots)), dma((2, spots)),
            dma((2, blocks)), dma((2, blocks)), dma((2,)),
            dma((2, blocks)), dma((2, blocks)), dma((owners,)), dma((n,)), dma((n,)), dma((owners,)),
        ],
        compiler_params=pltpu.CompilerParams(
            collective_id=0, has_side_effects=True, vmem_limit_bytes=60 * 1024 * 1024
        ),
        name="residual_blocks",
    )(
        owner, neighbours.T,
        features.reshape(slots, PIX, chans), out_cotangent.reshape(slots, PIX, chans),
        jnp.swapaxes(w_reduce, 1, 2), jnp.swapaxes(w_taps, 1, 2), w_expand, norm_scale, norm_shift,
        *consts,
    )
    shape = (1, slots, side, side, chans)
    return (
        results[0].reshape(shape), results[1].reshape(shape),
        jnp.swapaxes(results[2], 1, 2), jnp.swapaxes(results[3], 1, 2), results[4],
    )


def solution(mesh):
    return jax.shard_map(
        on_device,
        mesh=mesh,
        in_specs=(
            P("tile", None, None, None),
            P("tile", None, None, None),
            P("section", None, None),
            P("section", None, None),
            P("section", None, None),
            P("section", None),
            P("section", None),
            P(),
            P(),
        ),
        out_specs=(
            P("section", "tile", None, None, None),
            P("section", "tile", None, None, None),
            P("section", None, None),
            P("section", None, None),
            P("section", None, None),
        ),
        check_vma=False,
    )
```

```python
from functools import partial

import jax
import jax.numpy as jnp
import numpy as np
from jax import lax
from jax.experimental import pallas as pl
from jax.experimental.pallas import tpu as pltpu
from jax.sharding import PartitionSpec as P

REACH = 3
SPAN = 2 * REACH + 1
MESH = pl.DeviceIdType.MESH
SIDE = 16
PIX = SIDE * SIDE
EXT = PIX + 2 * SIDE
FULL = EXT + 2 * SIDE
REGIONS = (416, 128)


def shift_matrices():
    left = np.zeros((EXT, FULL), np.float32)
    right = np.zeros((EXT, FULL), np.float32)
    for r in range(EXT):
        y, x = r // SIDE - 1, r % SIDE
        inside = 0 <= y < SIDE
        if x > 0:
            left[r, r - 1] = 1
        elif inside:
            left[r, EXT + y] = 1
        if x < SIDE - 1:
            right[r, r + 1] = 1
        elif inside:
            right[r, EXT + SIDE + y] = 1
    face = np.zeros((4 * SIDE, PIX), np.float32)
    for i in range(SIDE):
        face[i, i] = 1
        face[SIDE + i, PIX - SIDE + i] = 1
        face[2 * SIDE + i, SIDE * i] = 1
        face[3 * SIDE + i, SIDE * i + SIDE - 1] = 1
    return np.concatenate([left, right]), face


def sigmoid(v):
    return 0.5 * jnp.tanh(0.5 * v) + 0.5


def mm(left, right):
    return jnp.dot(left, right, preferred_element_type=jnp.float32)


def mm_t(left, right):
    return lax.dot_general(
        left, right, (((1,), (1,)), ((), ())), preferred_element_type=jnp.float32
    )


def t_mm(left, right):
    return lax.dot_general(
        left, right, (((0,), (0,)), ((), ())), preferred_element_type=jnp.float32
    )


def kernel(
    n, blocks, chunks, counts,
    owner_ref, near_ref, feat_ref, cot_ref, w1_ref, wt_ref, w3_ref, sc_ref, sh_ref,
    inner_in, rim_in, inner_t_in, rim_t_in, face_in, face_t_in,
    out_ref, din_ref, gr_ref, gt_ref, ge_ref,
    sel, inner_ref, rim_ref, inner_t_ref, rim_t_ref, face_ref, face_t_ref, acts, dins, W1, WT, W3, WC, NS, NT,
    D1, D2, D3, pre2_s, pre3_s, CAT, H2, DD3, F, SEND, RECV, HELD, G0, G1, RS0, RS1, PART0, PART1, SG0, SG1, FIN0, FIN1,
    load_sem, const_sem, wl_sem, ws_sem, wr_sem, xs_sem, xr_sem,
    os_sem, or_sem, ol_sem, *grad_sems,
):
    s = lax.axis_index("section")
    k = lax.axis_index("tile")
    lo = jnp.maximum(k - REACH, 0)
    hi = jnp.minimum(k + REACH + 1, n)
    bf = jnp.bfloat16

    feat_copy = pltpu.make_async_copy(feat_ref.at[s], acts.at[0], load_sem.at[0])
    cot_copy = pltpu.make_async_copy(cot_ref.at[s], dins.at[blocks], load_sem.at[1])
    const_copies = [
        pltpu.make_async_copy(src, dst, const_sem.at[i])
        for i, (src, dst) in enumerate([
            (face_in, face_ref), (inner_in, inner_ref), (rim_in, rim_ref),
            (inner_t_in, inner_t_ref), (rim_t_in, rim_t_ref), (face_t_in, face_t_ref),
        ])
    ]
    feat_copy.start()
    weights = [
        (w1_ref.at[0], W1), (sc_ref, NS), (sh_ref, NT), (wt_ref.at[0], WT), (w3_ref.at[0], W3)
    ]
    for i, (src, dst) in enumerate(weights):
        pltpu.make_async_copy(src, dst.at[s], wl_sem.at[i]).start()
    for copy in const_copies:
        copy.start()
    cot_copy.start()

    barrier = pltpu.get_barrier_semaphore()

    def greet(kk, total):
        near = jnp.logical_and(kk >= lo, kk < hi)
        for ss in range(blocks):
            go = jnp.logical_and(
                jnp.logical_or(near, s == ss), jnp.logical_not(jnp.logical_and(s == ss, kk == k))
            )

            @pl.when(go)
            def _():
                pl.semaphore_signal(barrier, inc=1, device_id=(ss, kk), device_id_type=MESH)

        return total

    lax.fori_loop(0, n, greet, 0)
    slot = k * blocks + s
    tiles = owner_ref.shape[0]
    tile = lax.fori_loop(
        0, tiles, lambda i, acc: jnp.where(owner_ref[i] == slot, i, acc), jnp.int32(0)
    )
    places, valids = [], []
    for j in range(4):
        near = near_ref[j, tile]
        valid = near >= 0
        where = owner_ref[jnp.where(valid, near, 0)]
        hop = lax.rem(where % blocks - s + blocks, blocks)
        place = (where // blocks - k + REACH) * blocks + hop
        place = jnp.where(valid, place, 0)
        places.append(jnp.clip(place, 0, SPAN * blocks - 1))
        valids.append(valid)
    for i in range(SPAN * blocks):
        pick = jnp.int32(0)
        for j in range(1, 4):
            pick = jnp.where(jnp.logical_and(valids[j], places[j] == i), j, pick)
        sel[i] = pick

    pl.semaphore_wait(barrier, (hi - lo) * (blocks - 1) + n - 1)

    def weight_copy(i, target, slot):
        src, dst = weights[i]
        return pltpu.make_async_remote_copy(
            src_ref=src, dst_ref=dst.at[slot],
            send_sem=ws_sem.at[i, target], recv_sem=wr_sem.at[i, slot],
            device_id=(target, k), device_id_type=MESH,
        )

    def send_weights():
        for i in range(len(weights)):
            for target in range(blocks):
                @pl.when(s != target)
                def _():
                    weight_copy(i, target, s).start()

    @pl.when(s == 0)
    def _():
        send_weights()

    def partners():
        for far in sorted(range(-REACH, REACH + 1), key=lambda o: -abs(o)):
            yield far, [hop for hop in range(blocks) if far or hop]

    def exchange_copy(par, far, hop):
        theirs = (far + REACH) * blocks + hop
        mine = (REACH - far) * blocks + (blocks - hop) % blocks
        return pltpu.make_async_remote_copy(
            src_ref=SEND.at[par, theirs], dst_ref=RECV.at[par, mine],
            send_sem=xs_sem.at[par, theirs], recv_sem=xr_sem.at[par, mine],
            device_id=(lax.rem(s + hop, blocks), k + far), device_id_type=MESH,
        )

    def each_partner(action):
        for far, hops in partners():
            def body():
                for hop in hops:
                    action(far, hop)

            if far:
                pl.when(jnp.logical_and(k + far >= 0, k + far < n))(body)
            else:
                body()

    def sent(par):
        each_partner(lambda far, hop: exchange_copy(par, far, hop).wait_send())

    def start_exchange(par, faces):
        F[...] = jnp.concatenate([faces, faces], axis=1).reshape(4, SIDE, 128)
        for i in range(SPAN * blocks):
            SEND[par, i] = F[sel[i]]
        each_partner(lambda far, hop: exchange_copy(par, far, hop).start())

    def end_exchange(par):
        each_partner(lambda far, hop: exchange_copy(par, -far, -hop % blocks).wait_recv())
        HELD[...] = RECV[par]
        got = []
        for j in range(4):
            face = HELD[places[j]][:, :64]
            got.append(jnp.where(valids[j], face.astype(jnp.float32), 0.0).astype(bf))
        return got

    def result_copy(which, b, ref, src):
        return pltpu.make_async_remote_copy(
            src_ref=src, dst_ref=ref.at[s],
            send_sem=os_sem.at[which, b], recv_sem=or_sem.at[which, s],
            device_id=(b, k), device_id_type=MESH,
        )

    def result_local(which, ref, src):
        return pltpu.make_async_copy(src, ref.at[s], ol_sem.at[which])

    def send_result(which, b, ref, src):
        @pl.when(b != s)
        def _():
            result_copy(which, b, ref, src).start()

        @pl.when(b == s)
        def _():
            result_local(which, ref, src).start()

    def derivative(v):
        sig = sigmoid(v)
        return sig * (1.0 + v * (1.0 - sig))

    def tail_derivatives(b):
        D2[b] = derivative(pre2_s[...]) * NS[b][:, 64:128]
        D3[b] = derivative(pre3_s[...])

    for i, (src, dst) in enumerate(weights):
        pltpu.make_async_copy(src, dst.at[s], wl_sem.at[i]).wait()
    feat_copy.wait()
    for copy in const_copies:
        copy.wait()

    def forward(b, carry):
        par = lax.rem(b, 2)

        @pl.when(b != s)
        def _():
            for i in range(len(weights)):
                weight_copy(i, b, b).wait_recv()

        a = acts[b]
        scale = NS[b]
        shift = NT[b]
        pre1 = mm_t(a, W1[b]) * scale[:, :64] + shift[:, :64]
        sig = sigmoid(pre1)
        h1 = (pre1 * sig).astype(bf)
        start_exchange(par, mm(face_ref[...], h1).astype(bf))

        @pl.when(b > 0)
        def _():
            sent(1 - par)
            send_result(0, b - 1, out_ref, acts.at[b])
            tail_derivatives(b - 1)

        @pl.when(jnp.logical_and(b == 0, s != 0))
        def _():
            send_weights()

        D1[b] = sig * (1.0 + pre1 * (1.0 - sig)) * scale[:, :64]
        taps = WT[b]
        WC[b] = jnp.concatenate([taps[:, :192], taps[:, 192:384], taps[:, 384:]], axis=0)
        moved = mm(inner_ref[...], h1)

        got = end_exchange(par)
        full = jnp.concatenate([got[0], h1, got[1]], axis=0)
        moved = (moved + mm(rim_ref[...], jnp.concatenate(got, axis=0))).astype(bf)
        cat = jnp.concatenate([moved[:EXT], full, moved[EXT:]], axis=1)
        CAT[b] = cat
        rows = mm_t(cat, WC[b])
        pre2 = (
            rows[:PIX, :64] + rows[SIDE : SIDE + PIX, 64:128] + rows[2 * SIDE :, 128:]
        )
        pre2 = pre2 * scale[:, 64:128] + shift[:, 64:128]
        pre2_s[...] = pre2
        h2 = (pre2 * sigmoid(pre2)).astype(bf)
        H2[b] = h2
        pre3 = a.astype(jnp.float32) + mm(h2, W3[b]) * scale[:, 128:] + shift[:, 128:]
        pre3_s[...] = pre3
        acts[b + 1] = (pre3 * sigmoid(pre3)).astype(bf)
        return carry

    lax.fori_loop(0, blocks, forward, 0)
    tail_derivatives(blocks - 1)
    cot_copy.wait()

    grads = [
        (G0, RS0, PART0, SG0, FIN0, chunks[0], counts[0]) + grad_sems[:6],
        (G1, RS1, PART1, SG1, FIN1, chunks[1], counts[1]) + grad_sems[6:],
    ]

    def others(count, action):
        def body(kk, carry):
            @pl.when(kk != k)
            def _():
                action(kk)

            return carry

        lax.fori_loop(0, count, body, 0)

    def piece(r, b, kk):
        chunk = grads[r][5]
        return grads[r][0].at[b, pl.ds(pl.multiple_of(kk * chunk, 16), chunk)]

    def to_owner(r, b, kk):
        return pltpu.make_async_remote_copy(
            src_ref=piece(r, b, kk), dst_ref=grads[r][1].at[b, k],
            send_sem=grads[r][7].at[b, kk], recv_sem=grads[r][8].at[b, k],
            device_id=(s, kk), device_id_type=MESH,
        )

    def from_peer(r, b, kk):
        slot = grads[r][1].at[b, kk]
        return pltpu.make_async_remote_copy(
            src_ref=slot, dst_ref=slot,
            send_sem=grads[r][7].at[b, 0], recv_sem=grads[r][8].at[b, kk],
            device_id=(s, kk), device_id_type=MESH,
        )

    def to_section(r, b, slot):
        return pltpu.make_async_remote_copy(
            src_ref=grads[r][2].at[b], dst_ref=grads[r][3].at[slot],
            send_sem=grads[r][9].at[b], recv_sem=grads[r][10].at[slot],
            device_id=(b, k), device_id_type=MESH,
        )

    def final_copy(r, kk, slot):
        return pltpu.make_async_remote_copy(
            src_ref=grads[r][4].at[slot], dst_ref=grads[r][4].at[slot],
            send_sem=grads[r][11].at[kk], recv_sem=grads[r][12].at[slot],
            device_id=(s, kk), device_id_type=MESH,
        )

    def scatter(r, b):
        others(counts[r], lambda kk: to_owner(r, b, kk).start())

    def owner_sum(r, b):
        G, RS, PART, SG = grads[r][:4]
        chunk = chunks[r]

        @pl.when(k < counts[r])
        def _():
            RS[b, k] = G[b, pl.ds(pl.multiple_of(k * chunk, 16), chunk)]
            others(n, lambda kk: from_peer(r, b, kk).wait_recv())
            total = lax.fori_loop(
                0, n, lambda i, acc: acc + RS[b, i].astype(jnp.float32),
                jnp.zeros((chunk, 128), jnp.float32),
            ).astype(bf)

            @pl.when(b == s)
            def _():
                SG[s] = total

            @pl.when(b != s)
            def _():
                PART[b] = total
                to_section(r, b, s).start()

    def backward(step, carry):
        b = blocks - 1 - step
        par = lax.rem(step + blocks, 2)
        scale = NS[b]
        d3 = dins[b + 1].astype(jnp.float32) * D3[b]
        DD3[...] = d3
        e3 = (d3 * scale[:, 128:]).astype(bf)
        d2 = (mm_t(e3, W3[b]) * D2[b]).astype(bf)
        zero = jnp.zeros((SIDE, 64), bf)
        d2cat = jnp.concatenate(
            [
                jnp.concatenate([d2, zero, zero], axis=0),
                jnp.concatenate([zero, d2, zero], axis=0),
                jnp.concatenate([zero, zero, d2], axis=0),
            ],
            axis=1,
        )
        dcat = mm(d2cat, WC[b])
        sides = jnp.concatenate([dcat[:, :64], dcat[:, 128:]], axis=0).astype(bf)
        drim = mm(rim_t_ref[...], sides)
        mid = dcat[:, 64:128]
        faces = jnp.concatenate(
            [drim[:SIDE] + mid[:SIDE], drim[SIDE : 2 * SIDE] + mid[SIDE + PIX :], drim[2 * SIDE :]],
            axis=0,
        )
        start_exchange(par, faces.astype(bf))
        dmid = (mm(inner_t_ref[...], sides) + mid[SIDE : SIDE + PIX]).astype(bf)
        taps = t_mm(d2cat, CAT[b]).astype(bf)
        G0[b, :192] = taps[:, :128]
        G0[b, 192:288] = jnp.concatenate([taps[:96, 128:], taps[96:, 128:]], axis=1)
        expand = t_mm(H2[b], e3).astype(bf)
        G0[b, 288:352] = expand[:, :128]
        G0[b, 352:416] = expand[:, 128:]
        spare = counts[0] * chunks[0] - REGIONS[0]
        if spare:
            G0[b, REGIONS[0] :] = jnp.zeros((spare, 128), bf)
        scatter(0, b)
        sent(1 - par)

        @pl.when(step == 0)
        def _():
            send_result(0, blocks - 1, out_ref, acts.at[blocks])

        @pl.when(step > 0)
        def _():
            send_result(1, b + 1, din_ref, dins.at[b + 1])
            owner_sum(0, b + 1)
            owner_sum(1, b + 1)

        got = end_exchange(par)
        dh1 = dmid.astype(jnp.float32) + mm(
            face_t_ref[...], jnp.concatenate(got, axis=0)
        )
        d1 = (dh1 * D1[b]).astype(bf)
        red = t_mm(d1, acts[b]).astype(bf)
        G1[b, :64] = red[:, :128]
        G1[b, 64:] = red[:, 128:]
        scatter(1, b)
        dins[b] = (DD3[...] + mm(d1, W1[b])).astype(bf)
        return carry

    lax.fori_loop(0, blocks, backward, 0)
    send_result(1, 0, din_ref, dins.at[0])
    sent((2 * blocks - 1) % 2)

    for r in (0, 1):
        owner_sum(r, 0)
    for r in (0, 1):
        SG, FIN = grads[r][3:5]

        @pl.when(k < counts[r])
        def _():
            for ss in range(blocks):
                @pl.when(s != ss)
                def _():
                    to_section(r, ss, ss).wait_recv()

            FIN[k] = sum(SG[ss].astype(jnp.float32) for ss in range(blocks)).astype(bf)
            others(n, lambda kk: final_copy(r, kk, k).start())

    for r in (0, 1):
        others(counts[r], lambda kk: final_copy(r, kk, kk).wait_recv())
    done = FIN0[...].reshape(counts[0] * chunks[0], 128).astype(jnp.float32)
    red = FIN1[...].reshape(REGIONS[1], 128).astype(jnp.float32)
    right = jnp.concatenate([done[192:288, :64], done[192:288, 64:]], axis=0)
    for dy in range(3):
        span = slice(64 * dy, 64 * dy + 64)
        gt_ref[0, :, 192 * dy : 192 * dy + 192] = jnp.concatenate(
            [done[span], right[span]], axis=1
        )
    ge_ref[0, :, :128] = done[288:352]
    ge_ref[0, :, 128:] = done[352:416]
    gr_ref[0, :, :128] = red[:64]
    gr_ref[0, :, 128:] = red[64:]

    for r in (0, 1):
        for b in range(blocks):
            others(counts[r], lambda kk: to_owner(r, b, kk).wait_send())

        @pl.when(k < counts[r])
        def _():
            others(n, lambda kk: final_copy(r, kk, k).wait_send())
            for ss in range(blocks):
                @pl.when(s != ss)
                def _():
                    to_section(r, ss, ss).wait_send()

    for ss in range(blocks):
        @pl.when(s != ss)
        def _():
            for i in range(len(weights)):
                weight_copy(i, ss, ss).wait_send()
            for which, ref, held in ((0, out_ref, acts.at[ss + 1]), (1, din_ref, dins.at[ss])):
                pltpu.make_async_remote_copy(
                    src_ref=held, dst_ref=ref.at[ss],
                    send_sem=os_sem.at[which, ss], recv_sem=or_sem.at[which, ss],
                    device_id=(ss, k), device_id_type=MESH,
                ).wait()

    result_local(0, out_ref, acts.at[s + 1]).wait()
    result_local(1, din_ref, dins.at[s]).wait()


def copy_out(*refs):
    sems = refs[10]
    copies = [pltpu.make_async_copy(refs[i], refs[5 + i], sems.at[i]) for i in range(5)]
    for copy in copies:
        copy.start()
    for copy in copies:
        copy.wait()


def on_device(
    features, out_cotangent, w_reduce, w_taps, w_expand, norm_scale, norm_shift, owner, neighbours
):
    blocks = lax.axis_size("section")
    n = lax.axis_size("tile")
    slots, side, _, chans = features.shape
    bf, f32 = jnp.bfloat16, jnp.float32
    chunks = [16 * max(1, -(-rows // (16 * n))) for rows in REGIONS]
    counts = [-(-rows // chunk) for rows, chunk in zip(REGIONS, chunks)]
    shift, face = shift_matrices()
    inner = shift[:, SIDE : SIDE + PIX]
    rim = np.concatenate([shift[:, :SIDE], shift[:, SIDE + PIX :]], axis=1)
    consts = [jnp.asarray(m, bf) for m in (inner, rim, inner.T, rim.T, face, face.T)]
    vmem = pl.BlockSpec(memory_space=pltpu.VMEM)
    smem = pl.BlockSpec(memory_space=pltpu.SMEM)
    anyw = pl.BlockSpec(memory_space=pl.ANY)
    hbm = pl.BlockSpec(memory_space=pltpu.HBM)
    dma = pltpu.SemaphoreType.DMA
    spots = SPAN * blocks
    results = pl.pallas_call(
        partial(kernel, n, blocks, chunks, counts),
        out_shape=(
            jax.ShapeDtypeStruct((slots, PIX, chans), bf),
            jax.ShapeDtypeStruct((slots, PIX, chans), bf),
            jax.ShapeDtypeStruct((1, 64, 256), f32),
            jax.ShapeDtypeStruct((1, 64, 576), f32),
            jax.ShapeDtypeStruct((1, 64, 256), f32),
        ),
        in_specs=[smem] * 2 + [hbm] * 13,
        out_specs=[anyw] * 2 + [vmem] * 3,
        scratch_shapes=[
            pltpu.SMEM((spots,), jnp.int32),
            *[pltpu.VMEM(m.shape, bf) for m in consts],
            pltpu.VMEM((blocks + 1, PIX, chans), bf),
            pltpu.VMEM((blocks + 1, PIX, chans), bf),
            pltpu.VMEM((blocks, 64, 256), bf),
            pltpu.VMEM((blocks, 64, 576), bf),
            pltpu.VMEM((blocks, 64, 256), bf),
            pltpu.VMEM((blocks, 192, 192), bf),
            pltpu.VMEM((blocks, 1, 384), f32),
            pltpu.VMEM((blocks, 1, 384), f32),
            pltpu.VMEM((blocks, PIX, 64), f32),
            pltpu.VMEM((blocks, PIX, 64), f32),
            pltpu.VMEM((blocks, PIX, chans), f32),
            pltpu.VMEM((PIX, 64), f32),
            pltpu.VMEM((PIX, chans), f32),
            pltpu.VMEM((blocks, EXT, 192), bf),
            pltpu.VMEM((blocks, PIX, 64), bf),
            pltpu.VMEM((PIX, chans), f32),
            pltpu.VMEM((4, SIDE, 128), bf),
            pltpu.VMEM((2, spots, SIDE, 128), bf),
            pltpu.VMEM((2, spots, SIDE, 128), bf),
            pltpu.VMEM((spots, SIDE, 128), bf),
            *[pltpu.VMEM((blocks, c * m, 128), bf) for c, m in zip(chunks, counts)],
            *[pltpu.VMEM((blocks, n, c, 128), bf) for c in chunks],
            *[pltpu.VMEM((blocks, c, 128), bf) for c in chunks],
            *[pltpu.VMEM((blocks, c, 128), bf) for c in chunks],
            *[pltpu.VMEM((m, c, 128), bf) for c, m in zip(chunks, counts)],
            dma((2,)), dma((6,)), dma((5,)), dma((5, blocks)), dma((5, blocks)),
            dma((2, spots)), dma((2, spots)),
            dma((2, blocks)), dma((2, blocks)), dma((2,)),
            *[
                dma(shape)
                for m in counts
                for shape in ((blocks, m), (blocks, n), (blocks,), (blocks,), (n,), (m,))
            ],
        ],
        compiler_params=pltpu.CompilerParams(
            collective_id=0, has_side_effects=True, vmem_limit_bytes=60 * 1024 * 1024
        ),
        name="residual_blocks",
    )(
        owner, neighbours.T,
        features.reshape(slots, PIX, chans), out_cotangent.reshape(slots, PIX, chans),
        jnp.swapaxes(w_reduce, 1, 2), jnp.swapaxes(w_taps, 1, 2), w_expand, norm_scale, norm_shift,
        *consts,
    )
    results = pl.pallas_call(
        copy_out,
        out_shape=tuple(jax.ShapeDtypeStruct(r.shape, r.dtype) for r in results),
        in_specs=[anyw] * 5,
        out_specs=[anyw] * 5,
        scratch_shapes=[dma((5,))],
        name="copy_out",
    )(*results)
    shape = (1, slots, side, side, chans)
    return (
        results[0].reshape(shape), results[1].reshape(shape),
        jnp.swapaxes(results[2], 1, 2), jnp.swapaxes(results[3], 1, 2), results[4],
    )


def solution(mesh):
    return jax.shard_map(
        on_device,
        mesh=mesh,
        in_specs=(
            P("tile", None, None, None),
            P("tile", None, None, None),
            P("section", None, None),
            P("section", None, None),
            P("section", None, None),
            P("section", None),
            P("section", None),
            P(),
            P(),
        ),
        out_specs=(
            P("section", "tile", None, None, None),
            P("section", "tile", None, None, None),
            P("section", None, None),
            P("section", None, None),
            P("section", None, None),
        ),
        check_vma=False,
    )
```

```python
from functools import partial

import jax
import jax.numpy as jnp
import numpy as np
from jax import lax
from jax.experimental import pallas as pl
from jax.experimental.pallas import tpu as pltpu
from jax.sharding import PartitionSpec as P

REACH = 3
SPAN = 2 * REACH + 1
MESH = pl.DeviceIdType.MESH
SIDE = 16
PIX = SIDE * SIDE
EXT = PIX + 2 * SIDE
FULL = EXT + 2 * SIDE
REGIONS = (416, 128)


def shift_matrices():
    left = np.zeros((EXT, FULL), np.float32)
    right = np.zeros((EXT, FULL), np.float32)
    for r in range(EXT):
        y, x = r // SIDE - 1, r % SIDE
        inside = 0 <= y < SIDE
        if x > 0:
            left[r, r - 1] = 1
        elif inside:
            left[r, EXT + y] = 1
        if x < SIDE - 1:
            right[r, r + 1] = 1
        elif inside:
            right[r, EXT + SIDE + y] = 1
    face = np.zeros((4 * SIDE, PIX), np.float32)
    for i in range(SIDE):
        face[i, i] = 1
        face[SIDE + i, PIX - SIDE + i] = 1
        face[2 * SIDE + i, SIDE * i] = 1
        face[3 * SIDE + i, SIDE * i + SIDE - 1] = 1
    return np.concatenate([left, right]), face


def sigmoid(v):
    return 0.5 * jnp.tanh(0.5 * v) + 0.5


def mm(left, right):
    return jnp.dot(left, right, preferred_element_type=jnp.float32)


def mm_t(left, right):
    return lax.dot_general(
        left, right, (((1,), (1,)), ((), ())), preferred_element_type=jnp.float32
    )


def t_mm(left, right):
    return lax.dot_general(
        left, right, (((0,), (0,)), ((), ())), preferred_element_type=jnp.float32
    )


def kernel(
    n, blocks, chunks, counts,
    owner_ref, near_ref, feat_ref, cot_ref, w1_ref, wt_ref, w3_ref, sc_ref, sh_ref,
    inner_in, rim_in, inner_t_in, rim_t_in, face_in, face_t_in,
    out_ref, din_ref, gr_ref, gt_ref, ge_ref,
    sel, inner_ref, rim_ref, inner_t_ref, rim_t_ref, face_ref, face_t_ref, acts, dins, W1, WT, W3, WC, NS, NT,
    D1, D2, D3, pre2_s, pre3_s, CAT, H2, DD3, F, SEND, RECV, HELD, G0, G1, RS0, RS1, PART0, PART1, SG0, SG1, FIN0, FIN1,
    load_sem, const_sem, wl_sem, ws_sem, wr_sem, xs_sem, xr_sem,
    os_sem, or_sem, ol_sem, *grad_sems,
):
    s = lax.axis_index("section")
    k = lax.axis_index("tile")
    lo = jnp.maximum(k - REACH, 0)
    hi = jnp.minimum(k + REACH + 1, n)
    bf = jnp.bfloat16

    feat_copy = pltpu.make_async_copy(feat_ref.at[s], acts.at[0], load_sem.at[0])
    cot_copy = pltpu.make_async_copy(cot_ref.at[s], dins.at[blocks], load_sem.at[1])
    const_copies = [
        pltpu.make_async_copy(src, dst, const_sem.at[i])
        for i, (src, dst) in enumerate([
            (face_in, face_ref), (inner_in, inner_ref), (rim_in, rim_ref),
            (inner_t_in, inner_t_ref), (rim_t_in, rim_t_ref), (face_t_in, face_t_ref),
        ])
    ]
    feat_copy.start()
    weights = [
        (w1_ref.at[0], W1), (sc_ref, NS), (sh_ref, NT), (wt_ref.at[0], WT), (w3_ref.at[0], W3)
    ]
    for i, (src, dst) in enumerate(weights):
        pltpu.make_async_copy(src, dst.at[s], wl_sem.at[i]).start()
    for copy in const_copies:
        copy.start()
    cot_copy.start()

    barrier = pltpu.get_barrier_semaphore()

    def greet(kk, total):
        near = jnp.logical_and(kk >= lo, kk < hi)
        for ss in range(blocks):
            go = jnp.logical_and(
                jnp.logical_or(near, s == ss), jnp.logical_not(jnp.logical_and(s == ss, kk == k))
            )

            @pl.when(go)
            def _():
                pl.semaphore_signal(barrier, inc=1, device_id=(ss, kk), device_id_type=MESH)

        return total

    lax.fori_loop(0, n, greet, 0)
    slot = k * blocks + s
    tiles = owner_ref.shape[0]
    tile = lax.fori_loop(
        0, tiles, lambda i, acc: jnp.where(owner_ref[i] == slot, i, acc), jnp.int32(0)
    )
    places, valids = [], []
    for j in range(4):
        near = near_ref[j, tile]
        valid = near >= 0
        where = owner_ref[jnp.where(valid, near, 0)]
        hop = lax.rem(where % blocks - s + blocks, blocks)
        place = (where // blocks - k + REACH) * blocks + hop
        place = jnp.where(valid, place, 0)
        places.append(jnp.clip(place, 0, SPAN * blocks - 1))
        valids.append(valid)
    for i in range(SPAN * blocks):
        pick = jnp.int32(0)
        for j in range(1, 4):
            pick = jnp.where(jnp.logical_and(valids[j], places[j] == i), j, pick)
        sel[i] = pick

    pl.semaphore_wait(barrier, (hi - lo) * (blocks - 1) + n - 1)

    def weight_copy(i, target, slot):
        src, dst = weights[i]
        return pltpu.make_async_remote_copy(
            src_ref=src, dst_ref=dst.at[slot],
            send_sem=ws_sem.at[i, target], recv_sem=wr_sem.at[i, slot],
            device_id=(target, k), device_id_type=MESH,
        )

    def send_weights():
        for i in range(len(weights)):
            for target in range(blocks):
                @pl.when(s != target)
                def _():
                    weight_copy(i, target, s).start()

    @pl.when(s == 0)
    def _():
        send_weights()

    def partners():
        for far in sorted(range(-REACH, REACH + 1), key=lambda o: -abs(o)):
            yield far, [hop for hop in range(blocks) if far or hop]

    def exchange_copy(par, far, hop):
        theirs = (far + REACH) * blocks + hop
        mine = (REACH - far) * blocks + (blocks - hop) % blocks
        return pltpu.make_async_remote_copy(
            src_ref=SEND.at[par, theirs], dst_ref=RECV.at[par, mine],
            send_sem=xs_sem.at[par, theirs], recv_sem=xr_sem.at[par, mine],
            device_id=(lax.rem(s + hop, blocks), k + far), device_id_type=MESH,
        )

    def each_partner(action):
        for far, hops in partners():
            def body():
                for hop in hops:
                    action(far, hop)

            if far:
                pl.when(jnp.logical_and(k + far >= 0, k + far < n))(body)
            else:
                body()

    def sent(par):
        each_partner(lambda far, hop: exchange_copy(par, far, hop).wait_send())

    def start_exchange(par, faces):
        F[...] = jnp.concatenate([faces, faces], axis=1).reshape(4, SIDE, 128)
        for i in range(SPAN * blocks):
            SEND[par, i] = F[sel[i]]
        each_partner(lambda far, hop: exchange_copy(par, far, hop).start())

    def end_exchange(par):
        each_partner(lambda far, hop: exchange_copy(par, -far, -hop % blocks).wait_recv())
        HELD[...] = RECV[par]
        got = []
        for j in range(4):
            face = HELD[places[j]][:, :64]
            got.append(jnp.where(valids[j], face.astype(jnp.float32), 0.0).astype(bf))
        return got

    def result_copy(which, b, ref, src, half, slot):
        rows = pl.ds(half * (PIX // 2), PIX // 2)
        return pltpu.make_async_remote_copy(
            src_ref=src.at[rows], dst_ref=ref.at[slot, rows],
            send_sem=os_sem.at[which, b, half], recv_sem=or_sem.at[which, slot, half],
            device_id=(b, k), device_id_type=MESH,
        )

    def result_local(which, ref, src):
        return pltpu.make_async_copy(src, ref.at[s], ol_sem.at[which])

    def send_result(which, b, ref, src, halves=(0, 1)):
        @pl.when(b != s)
        def _():
            for half in halves:
                result_copy(which, b, ref, src, half, s).start()

        if 0 in halves:
            @pl.when(b == s)
            def _():
                result_local(which, ref, src).start()

    def derivative(v):
        sig = sigmoid(v)
        return sig * (1.0 + v * (1.0 - sig))

    def tail_derivatives(b):
        D2[b] = derivative(pre2_s[...]) * NS[b][:, 64:128]
        D3[b] = derivative(pre3_s[...])

    for i, (src, dst) in enumerate(weights):
        pltpu.make_async_copy(src, dst.at[s], wl_sem.at[i]).wait()
    feat_copy.wait()
    for copy in const_copies:
        copy.wait()

    def forward(b, carry):
        par = lax.rem(b, 2)

        @pl.when(b != s)
        def _():
            for i in range(len(weights)):
                weight_copy(i, b, b).wait_recv()

        a = acts[b]
        scale = NS[b]
        shift = NT[b]
        pre1 = mm_t(a, W1[b]) * scale[:, :64] + shift[:, :64]
        sig = sigmoid(pre1)
        h1 = (pre1 * sig).astype(bf)
        start_exchange(par, mm(face_ref[...], h1).astype(bf))

        @pl.when(b > 0)
        def _():
            sent(1 - par)
            send_result(0, b - 1, out_ref, acts.at[b])
            tail_derivatives(b - 1)

        @pl.when(jnp.logical_and(b == 0, s != 0))
        def _():
            send_weights()

        D1[b] = sig * (1.0 + pre1 * (1.0 - sig)) * scale[:, :64]
        taps = WT[b]
        WC[b] = jnp.concatenate([taps[:, :192], taps[:, 192:384], taps[:, 384:]], axis=0)
        moved = mm(inner_ref[...], h1)

        got = end_exchange(par)
        full = jnp.concatenate([got[0], h1, got[1]], axis=0)
        moved = (moved + mm(rim_ref[...], jnp.concatenate(got, axis=0))).astype(bf)
        cat = jnp.concatenate([moved[:EXT], full, moved[EXT:]], axis=1)
        CAT[b] = cat
        rows = mm_t(cat, WC[b])
        pre2 = (
            rows[:PIX, :64] + rows[SIDE : SIDE + PIX, 64:128] + rows[2 * SIDE :, 128:]
        )
        pre2 = pre2 * scale[:, 64:128] + shift[:, 64:128]
        pre2_s[...] = pre2
        h2 = (pre2 * sigmoid(pre2)).astype(bf)
        H2[b] = h2
        pre3 = a.astype(jnp.float32) + mm(h2, W3[b]) * scale[:, 128:] + shift[:, 128:]
        pre3_s[...] = pre3
        acts[b + 1] = (pre3 * sigmoid(pre3)).astype(bf)
        return carry

    lax.fori_loop(0, blocks, forward, 0)
    tail_derivatives(blocks - 1)
    cot_copy.wait()

    grads = [
        (G0, RS0, PART0, SG0, FIN0, chunks[0], counts[0]) + grad_sems[:6],
        (G1, RS1, PART1, SG1, FIN1, chunks[1], counts[1]) + grad_sems[6:],
    ]

    def others(count, action):
        def body(kk, carry):
            @pl.when(kk != k)
            def _():
                action(kk)

            return carry

        lax.fori_loop(0, count, body, 0)

    def piece(r, b, kk):
        chunk = grads[r][5]
        return grads[r][0].at[b, pl.ds(pl.multiple_of(kk * chunk, 16), chunk)]

    def to_owner(r, b, kk):
        return pltpu.make_async_remote_copy(
            src_ref=piece(r, b, kk), dst_ref=grads[r][1].at[b, k],
            send_sem=grads[r][7].at[b, kk], recv_sem=grads[r][8].at[b, k],
            device_id=(s, kk), device_id_type=MESH,
        )

    def from_peer(r, b, kk):
        slot = grads[r][1].at[b, kk]
        return pltpu.make_async_remote_copy(
            src_ref=slot, dst_ref=slot,
            send_sem=grads[r][7].at[b, 0], recv_sem=grads[r][8].at[b, kk],
            device_id=(s, kk), device_id_type=MESH,
        )

    def to_section(r, b, slot):
        return pltpu.make_async_remote_copy(
            src_ref=grads[r][2].at[b], dst_ref=grads[r][3].at[slot],
            send_sem=grads[r][9].at[b], recv_sem=grads[r][10].at[slot],
            device_id=(b, k), device_id_type=MESH,
        )

    def final_copy(r, kk, slot):
        return pltpu.make_async_remote_copy(
            src_ref=grads[r][4].at[slot], dst_ref=grads[r][4].at[slot],
            send_sem=grads[r][11].at[kk], recv_sem=grads[r][12].at[slot],
            device_id=(s, kk), device_id_type=MESH,
        )

    def scatter(r, b):
        others(counts[r], lambda kk: to_owner(r, b, kk).start())

    def owner_sum(r, b):
        G, RS, PART, SG = grads[r][:4]
        chunk = chunks[r]

        @pl.when(k < counts[r])
        def _():
            RS[b, k] = G[b, pl.ds(pl.multiple_of(k * chunk, 16), chunk)]
            others(n, lambda kk: from_peer(r, b, kk).wait_recv())
            total = lax.fori_loop(
                0, n, lambda i, acc: acc + RS[b, i].astype(jnp.float32),
                jnp.zeros((chunk, 128), jnp.float32),
            ).astype(bf)

            @pl.when(b == s)
            def _():
                SG[s] = total

            @pl.when(b != s)
            def _():
                PART[b] = total
                to_section(r, b, s).start()

    def backward(step, carry):
        b = blocks - 1 - step
        par = lax.rem(step + blocks, 2)
        scale = NS[b]
        d3 = dins[b + 1].astype(jnp.float32) * D3[b]
        DD3[...] = d3
        e3 = (d3 * scale[:, 128:]).astype(bf)
        d2 = (mm_t(e3, W3[b]) * D2[b]).astype(bf)
        zero = jnp.zeros((SIDE, 64), bf)
        d2cat = jnp.concatenate(
            [
                jnp.concatenate([d2, zero, zero], axis=0),
                jnp.concatenate([zero, d2, zero], axis=0),
                jnp.concatenate([zero, zero, d2], axis=0),
            ],
            axis=1,
        )
        dcat = mm(d2cat, WC[b])
        sides = jnp.concatenate([dcat[:, :64], dcat[:, 128:]], axis=0).astype(bf)
        drim = mm(rim_t_ref[...], sides)
        mid = dcat[:, 64:128]
        faces = jnp.concatenate(
            [drim[:SIDE] + mid[:SIDE], drim[SIDE : 2 * SIDE] + mid[SIDE + PIX :], drim[2 * SIDE :]],
            axis=0,
        )
        start_exchange(par, faces.astype(bf))
        dmid = (mm(inner_t_ref[...], sides) + mid[SIDE : SIDE + PIX]).astype(bf)
        taps = t_mm(d2cat, CAT[b]).astype(bf)
        G0[b, :192] = taps[:, :128]
        G0[b, 192:288] = jnp.concatenate([taps[:96, 128:], taps[96:, 128:]], axis=1)
        expand = t_mm(H2[b], e3).astype(bf)
        G0[b, 288:352] = expand[:, :128]
        G0[b, 352:416] = expand[:, 128:]
        spare = counts[0] * chunks[0] - REGIONS[0]
        if spare:
            G0[b, REGIONS[0] :] = jnp.zeros((spare, 128), bf)
        scatter(0, b)
        sent(1 - par)

        @pl.when(step == 0)
        def _():
            send_result(0, blocks - 1, out_ref, acts.at[blocks])

        @pl.when(step > 0)
        def _():
            send_result(1, b + 1, din_ref, dins.at[b + 1])
            owner_sum(0, b + 1)
            owner_sum(1, b + 1)

        got = end_exchange(par)
        dh1 = dmid.astype(jnp.float32) + mm(
            face_t_ref[...], jnp.concatenate(got, axis=0)
        )
        d1 = (dh1 * D1[b]).astype(bf)
        red = t_mm(d1, acts[b]).astype(bf)
        G1[b, :64] = red[:, :128]
        G1[b, 64:] = red[:, 128:]
        scatter(1, b)
        dins[b] = (DD3[...] + mm(d1, W1[b])).astype(bf)
        return carry

    lax.fori_loop(0, blocks, backward, 0)
    send_result(1, 0, din_ref, dins.at[0], (0,))
    sent((2 * blocks - 1) % 2)

    for r in (0, 1):
        owner_sum(r, 0)
    send_result(1, 0, din_ref, dins.at[0], (1,))
    for r in (0, 1):
        SG, FIN = grads[r][3:5]

        @pl.when(k < counts[r])
        def _():
            for ss in range(blocks):
                @pl.when(s != ss)
                def _():
                    to_section(r, ss, ss).wait_recv()

            FIN[k] = sum(SG[ss].astype(jnp.float32) for ss in range(blocks)).astype(bf)
            others(n, lambda kk: final_copy(r, kk, k).start())

    for r in (0, 1):
        others(counts[r], lambda kk: final_copy(r, kk, kk).wait_recv())
    done = FIN0[...].reshape(counts[0] * chunks[0], 128).astype(jnp.float32)
    red = FIN1[...].reshape(REGIONS[1], 128).astype(jnp.float32)
    right = jnp.concatenate([done[192:288, :64], done[192:288, 64:]], axis=0)
    for dy in range(3):
        span = slice(64 * dy, 64 * dy + 64)
        gt_ref[0, :, 192 * dy : 192 * dy + 192] = jnp.concatenate(
            [done[span], right[span]], axis=1
        )
    ge_ref[0, :, :128] = done[288:352]
    ge_ref[0, :, 128:] = done[352:416]
    gr_ref[0, :, :128] = red[:64]
    gr_ref[0, :, 128:] = red[64:]

    for r in (0, 1):
        for b in range(blocks):
            others(counts[r], lambda kk: to_owner(r, b, kk).wait_send())

        @pl.when(k < counts[r])
        def _():
            others(n, lambda kk: final_copy(r, kk, k).wait_send())
            for ss in range(blocks):
                @pl.when(s != ss)
                def _():
                    to_section(r, ss, ss).wait_send()

    for ss in range(blocks):
        @pl.when(s != ss)
        def _():
            for i in range(len(weights)):
                weight_copy(i, ss, ss).wait_send()
            for which, ref, held in ((0, out_ref, acts.at[ss + 1]), (1, din_ref, dins.at[ss])):
                for half in (0, 1):
                    result_copy(which, ss, ref, held, half, ss).wait()

    result_local(0, out_ref, acts.at[s + 1]).wait()
    result_local(1, din_ref, dins.at[s]).wait()


def copy_out(*refs):
    held, load, store = refs[10:15], refs[15], refs[16]
    pieces = [
        (refs[i].at[part], held[i].at[part], refs[5 + i].at[part])
        for i in range(5)
        for part in range(refs[i].shape[0])
    ]
    loads = [pltpu.make_async_copy(p[0], p[1], load.at[i]) for i, p in enumerate(pieces)]
    stores = [pltpu.make_async_copy(p[1], p[2], store.at[i]) for i, p in enumerate(pieces)]
    for copy in loads:
        copy.start()
    for before, after in zip(loads, stores):
        before.wait()
        after.start()
    for copy in stores:
        copy.wait()


def on_device(
    features, out_cotangent, w_reduce, w_taps, w_expand, norm_scale, norm_shift, owner, neighbours
):
    blocks = lax.axis_size("section")
    n = lax.axis_size("tile")
    slots, side, _, chans = features.shape
    bf, f32 = jnp.bfloat16, jnp.float32
    chunks = [16 * max(1, -(-rows // (16 * n))) for rows in REGIONS]
    counts = [-(-rows // chunk) for rows, chunk in zip(REGIONS, chunks)]
    shift, face = shift_matrices()
    inner = shift[:, SIDE : SIDE + PIX]
    rim = np.concatenate([shift[:, :SIDE], shift[:, SIDE + PIX :]], axis=1)
    consts = [jnp.asarray(m, bf) for m in (inner, rim, inner.T, rim.T, face, face.T)]
    vmem = pl.BlockSpec(memory_space=pltpu.VMEM)
    smem = pl.BlockSpec(memory_space=pltpu.SMEM)
    anyw = pl.BlockSpec(memory_space=pl.ANY)
    hbm = pl.BlockSpec(memory_space=pltpu.HBM)
    dma = pltpu.SemaphoreType.DMA
    spots = SPAN * blocks
    results = pl.pallas_call(
        partial(kernel, n, blocks, chunks, counts),
        out_shape=(
            jax.ShapeDtypeStruct((slots, PIX, chans), bf),
            jax.ShapeDtypeStruct((slots, PIX, chans), bf),
            jax.ShapeDtypeStruct((1, 64, 256), f32),
            jax.ShapeDtypeStruct((1, 64, 576), f32),
            jax.ShapeDtypeStruct((1, 64, 256), f32),
        ),
        in_specs=[smem] * 2 + [hbm] * 13,
        out_specs=[anyw] * 2 + [vmem] * 3,
        scratch_shapes=[
            pltpu.SMEM((spots,), jnp.int32),
            *[pltpu.VMEM(m.shape, bf) for m in consts],
            pltpu.VMEM((blocks + 1, PIX, chans), bf),
            pltpu.VMEM((blocks + 1, PIX, chans), bf),
            pltpu.VMEM((blocks, 64, 256), bf),
            pltpu.VMEM((blocks, 64, 576), bf),
            pltpu.VMEM((blocks, 64, 256), bf),
            pltpu.VMEM((blocks, 192, 192), bf),
            pltpu.VMEM((blocks, 1, 384), f32),
            pltpu.VMEM((blocks, 1, 384), f32),
            pltpu.VMEM((blocks, PIX, 64), f32),
            pltpu.VMEM((blocks, PIX, 64), f32),
            pltpu.VMEM((blocks, PIX, chans), f32),
            pltpu.VMEM((PIX, 64), f32),
            pltpu.VMEM((PIX, chans), f32),
            pltpu.VMEM((blocks, EXT, 192), bf),
            pltpu.VMEM((blocks, PIX, 64), bf),
            pltpu.VMEM((PIX, chans), f32),
            pltpu.VMEM((4, SIDE, 128), bf),
            pltpu.VMEM((2, spots, SIDE, 128), bf),
            pltpu.VMEM((2, spots, SIDE, 128), bf),
            pltpu.VMEM((spots, SIDE, 128), bf),
            *[pltpu.VMEM((blocks, c * m, 128), bf) for c, m in zip(chunks, counts)],
            *[pltpu.VMEM((blocks, n, c, 128), bf) for c in chunks],
            *[pltpu.VMEM((blocks, c, 128), bf) for c in chunks],
            *[pltpu.VMEM((blocks, c, 128), bf) for c in chunks],
            *[pltpu.VMEM((m, c, 128), bf) for c, m in zip(chunks, counts)],
            dma((2,)), dma((6,)), dma((5,)), dma((5, blocks)), dma((5, blocks)),
            dma((2, spots)), dma((2, spots)),
            dma((2, blocks, 2)), dma((2, blocks, 2)), dma((2,)),
            *[
                dma(shape)
                for m in counts
                for shape in ((blocks, m), (blocks, n), (blocks,), (blocks,), (n,), (m,))
            ],
        ],
        compiler_params=pltpu.CompilerParams(
            collective_id=0, has_side_effects=True, vmem_limit_bytes=60 * 1024 * 1024
        ),
        name="residual_blocks",
    )(
        owner, neighbours.T,
        features.reshape(slots, PIX, chans), out_cotangent.reshape(slots, PIX, chans),
        jnp.swapaxes(w_reduce, 1, 2), jnp.swapaxes(w_taps, 1, 2), w_expand, norm_scale, norm_shift,
        *consts,
    )
    results = pl.pallas_call(
        copy_out,
        out_shape=tuple(jax.ShapeDtypeStruct(r.shape, r.dtype) for r in results),
        in_specs=[anyw] * 5,
        out_specs=[anyw] * 5,
        scratch_shapes=[
            *[pltpu.VMEM(r.shape, r.dtype) for r in results],
            dma((2 * slots + 3,)), dma((2 * slots + 3,)),
        ],
        name="copy_out",
    )(*results)
    shape = (1, slots, side, side, chans)
    return (
        results[0].reshape(shape), results[1].reshape(shape),
        jnp.swapaxes(results[2], 1, 2), jnp.swapaxes(results[3], 1, 2), results[4],
    )


def solution(mesh):
    return jax.shard_map(
        on_device,
        mesh=mesh,
        in_specs=(
            P("tile", None, None, None),
            P("tile", None, None, None),
            P("section", None, None),
            P("section", None, None),
            P("section", None, None),
            P("section", None),
            P("section", None),
            P(),
            P(),
        ),
        out_specs=(
            P("section", "tile", None, None, None),
            P("section", "tile", None, None, None),
            P("section", None, None),
            P("section", None, None),
            P("section", None, None),
        ),
        check_vma=False,
    )
```

```python
from functools import partial

import jax
import jax.numpy as jnp
import numpy as np
from jax import lax
from jax.experimental import pallas as pl
from jax.experimental.pallas import tpu as pltpu
from jax.sharding import PartitionSpec as P

REACH = 3
SPAN = 2 * REACH + 1
MESH = pl.DeviceIdType.MESH
SIDE = 16
PIX = SIDE * SIDE
EXT = PIX + 2 * SIDE
FULL = EXT + 2 * SIDE
REGIONS = (416, 128)


def shift_matrices():
    left = np.zeros((EXT, FULL), np.float32)
    right = np.zeros((EXT, FULL), np.float32)
    for r in range(EXT):
        y, x = r // SIDE - 1, r % SIDE
        inside = 0 <= y < SIDE
        if x > 0:
            left[r, r - 1] = 1
        elif inside:
            left[r, EXT + y] = 1
        if x < SIDE - 1:
            right[r, r + 1] = 1
        elif inside:
            right[r, EXT + SIDE + y] = 1
    face = np.zeros((4 * SIDE, PIX), np.float32)
    for i in range(SIDE):
        face[i, i] = 1
        face[SIDE + i, PIX - SIDE + i] = 1
        face[2 * SIDE + i, SIDE * i] = 1
        face[3 * SIDE + i, SIDE * i + SIDE - 1] = 1
    return np.concatenate([left, right]), face


def sigmoid(v):
    return 0.5 * jnp.tanh(0.5 * v) + 0.5


def mm(left, right):
    return jnp.dot(left, right, preferred_element_type=jnp.float32)


def mm_t(left, right):
    return lax.dot_general(
        left, right, (((1,), (1,)), ((), ())), preferred_element_type=jnp.float32
    )


def t_mm(left, right):
    return lax.dot_general(
        left, right, (((0,), (0,)), ((), ())), preferred_element_type=jnp.float32
    )


def kernel(
    n, blocks, chunks, counts,
    owner_ref, near_ref, feat_ref, cot_ref, w1_ref, wt_ref, w3_ref, sc_ref, sh_ref,
    inner_in, rim_in, inner_t_in, rim_t_in, face_in, face_t_in,
    out_ref, din_ref, gr_ref, gt_ref, ge_ref,
    sel, inner_ref, rim_ref, inner_t_ref, rim_t_ref, face_ref, face_t_ref, acts, dins, W1, WT, W3, WC, NS, NT,
    D1, D2, D3, pre2_s, pre3_s, CAT, H2, DD1, DD3, F, SEND, RECV, HELD, G0, G1, RS0, RS1, PART0, PART1, SG0, SG1, FIN0, FIN1,
    load_sem, const_sem, wl_sem, ws_sem, wr_sem, xs_sem, xr_sem,
    os_sem, or_sem, ol_sem, *grad_sems,
):
    s = lax.axis_index("section")
    k = lax.axis_index("tile")
    lo = jnp.maximum(k - REACH, 0)
    hi = jnp.minimum(k + REACH + 1, n)
    bf = jnp.bfloat16

    feat_copy = pltpu.make_async_copy(feat_ref.at[s], acts.at[0], load_sem.at[0])
    cot_copy = pltpu.make_async_copy(cot_ref.at[s], dins.at[blocks], load_sem.at[1])
    const_copies = [
        pltpu.make_async_copy(src, dst, const_sem.at[i])
        for i, (src, dst) in enumerate([
            (face_in, face_ref), (inner_in, inner_ref), (rim_in, rim_ref),
            (inner_t_in, inner_t_ref), (rim_t_in, rim_t_ref), (face_t_in, face_t_ref),
        ])
    ]
    feat_copy.start()
    weights = [
        (w1_ref.at[0], W1), (sc_ref, NS), (sh_ref, NT), (wt_ref.at[0], WT), (w3_ref.at[0], W3)
    ]
    for i, (src, dst) in enumerate(weights):
        pltpu.make_async_copy(src, dst.at[s], wl_sem.at[i]).start()
    for copy in const_copies:
        copy.start()
    cot_copy.start()

    barrier = pltpu.get_barrier_semaphore()

    def greet(kk, total):
        near = jnp.logical_and(kk >= lo, kk < hi)
        for ss in range(blocks):
            go = jnp.logical_and(
                jnp.logical_or(near, s == ss), jnp.logical_not(jnp.logical_and(s == ss, kk == k))
            )

            @pl.when(go)
            def _():
                pl.semaphore_signal(barrier, inc=1, device_id=(ss, kk), device_id_type=MESH)

        return total

    lax.fori_loop(0, n, greet, 0)
    slot = k * blocks + s
    tiles = owner_ref.shape[0]
    tile = lax.fori_loop(
        0, tiles, lambda i, acc: jnp.where(owner_ref[i] == slot, i, acc), jnp.int32(0)
    )
    places, valids = [], []
    for j in range(4):
        near = near_ref[j, tile]
        valid = near >= 0
        where = owner_ref[jnp.where(valid, near, 0)]
        hop = lax.rem(where % blocks - s + blocks, blocks)
        place = (where // blocks - k + REACH) * blocks + hop
        place = jnp.where(valid, place, 0)
        places.append(jnp.clip(place, 0, SPAN * blocks - 1))
        valids.append(valid)
    for i in range(SPAN * blocks):
        pick = jnp.int32(0)
        for j in range(1, 4):
            pick = jnp.where(jnp.logical_and(valids[j], places[j] == i), j, pick)
        sel[i] = pick

    pl.semaphore_wait(barrier, (hi - lo) * (blocks - 1) + n - 1)

    def weight_copy(i, target, slot):
        src, dst = weights[i]
        return pltpu.make_async_remote_copy(
            src_ref=src, dst_ref=dst.at[slot],
            send_sem=ws_sem.at[i, target], recv_sem=wr_sem.at[i, slot],
            device_id=(target, k), device_id_type=MESH,
        )

    def send_weights():
        for i in range(len(weights)):
            for target in range(blocks):
                @pl.when(s != target)
                def _():
                    weight_copy(i, target, s).start()

    @pl.when(s == 0)
    def _():
        send_weights()

    def partners():
        for far in sorted(range(-REACH, REACH + 1), key=lambda o: -abs(o)):
            yield far, [hop for hop in range(blocks) if far or hop]

    def exchange_copy(par, far, hop):
        theirs = (far + REACH) * blocks + hop
        mine = (REACH - far) * blocks + (blocks - hop) % blocks
        return pltpu.make_async_remote_copy(
            src_ref=SEND.at[par, theirs], dst_ref=RECV.at[par, mine],
            send_sem=xs_sem.at[par, theirs], recv_sem=xr_sem.at[par, mine],
            device_id=(lax.rem(s + hop, blocks), k + far), device_id_type=MESH,
        )

    def each_partner(action):
        for far, hops in partners():
            def body():
                for hop in hops:
                    action(far, hop)

            if far:
                pl.when(jnp.logical_and(k + far >= 0, k + far < n))(body)
            else:
                body()

    def sent(par):
        each_partner(lambda far, hop: exchange_copy(par, far, hop).wait_send())

    def start_exchange(par, faces):
        F[...] = jnp.concatenate([faces, faces], axis=1).reshape(4, SIDE, 128)
        for i in range(SPAN * blocks):
            SEND[par, i] = F[sel[i]]
        each_partner(lambda far, hop: exchange_copy(par, far, hop).start())

    def end_exchange(par):
        each_partner(lambda far, hop: exchange_copy(par, -far, -hop % blocks).wait_recv())
        HELD[...] = RECV[par]
        got = []
        for j in range(4):
            face = HELD[places[j]][:, :64]
            got.append(jnp.where(valids[j], face.astype(jnp.float32), 0.0).astype(bf))
        return got

    def result_copy(which, b, ref, src, half, slot):
        rows = pl.ds(half * (PIX // 2), PIX // 2)
        return pltpu.make_async_remote_copy(
            src_ref=src.at[rows], dst_ref=ref.at[slot, rows],
            send_sem=os_sem.at[which, b, half], recv_sem=or_sem.at[which, slot, half],
            device_id=(b, k), device_id_type=MESH,
        )

    def result_local(which, ref, src):
        return pltpu.make_async_copy(src, ref.at[s], ol_sem.at[which])

    def send_result(which, b, ref, src, halves=(0, 1)):
        @pl.when(b != s)
        def _():
            for half in halves:
                result_copy(which, b, ref, src, half, s).start()

        if 0 in halves:
            @pl.when(b == s)
            def _():
                result_local(which, ref, src).start()

    def derivative(v):
        sig = sigmoid(v)
        return sig * (1.0 + v * (1.0 - sig))

    def tail_derivatives(b):
        D2[b] = derivative(pre2_s[...]) * NS[b][:, 64:128]
        D3[b] = derivative(pre3_s[...])

    for i, (src, dst) in enumerate(weights):
        pltpu.make_async_copy(src, dst.at[s], wl_sem.at[i]).wait()
    feat_copy.wait()
    for copy in const_copies:
        copy.wait()

    def forward(b, carry):
        par = lax.rem(b, 2)

        @pl.when(b != s)
        def _():
            for i in range(len(weights)):
                weight_copy(i, b, b).wait_recv()

        a = acts[b]
        scale = NS[b]
        shift = NT[b]
        pre1 = mm_t(a, W1[b]) * scale[:, :64] + shift[:, :64]
        sig = sigmoid(pre1)
        h1 = (pre1 * sig).astype(bf)
        start_exchange(par, mm(face_ref[...], h1).astype(bf))

        @pl.when(b > 0)
        def _():
            sent(1 - par)
            send_result(0, b - 1, out_ref, acts.at[b])
            tail_derivatives(b - 1)

        @pl.when(jnp.logical_and(b == 0, s != 0))
        def _():
            send_weights()

        D1[b] = sig * (1.0 + pre1 * (1.0 - sig)) * scale[:, :64]
        taps = WT[b]
        WC[b] = jnp.concatenate([taps[:, :192], taps[:, 192:384], taps[:, 384:]], axis=0)
        moved = mm(inner_ref[...], h1)

        got = end_exchange(par)
        full = jnp.concatenate([got[0], h1, got[1]], axis=0)
        moved = (moved + mm(rim_ref[...], jnp.concatenate(got, axis=0))).astype(bf)
        cat = jnp.concatenate([moved[:EXT], full, moved[EXT:]], axis=1)
        CAT[b] = cat
        rows = mm_t(cat, WC[b])
        pre2 = (
            rows[:PIX, :64] + rows[SIDE : SIDE + PIX, 64:128] + rows[2 * SIDE :, 128:]
        )
        pre2 = pre2 * scale[:, 64:128] + shift[:, 64:128]
        pre2_s[...] = pre2
        h2 = (pre2 * sigmoid(pre2)).astype(bf)
        H2[b] = h2
        pre3 = a.astype(jnp.float32) + mm(h2, W3[b]) * scale[:, 128:] + shift[:, 128:]
        pre3_s[...] = pre3
        acts[b + 1] = (pre3 * sigmoid(pre3)).astype(bf)
        return carry

    lax.fori_loop(0, blocks, forward, 0)
    tail_derivatives(blocks - 1)
    cot_copy.wait()

    grads = [
        (G0, RS0, PART0, SG0, FIN0, chunks[0], counts[0]) + grad_sems[:6],
        (G1, RS1, PART1, SG1, FIN1, chunks[1], counts[1]) + grad_sems[6:],
    ]

    def others(count, action):
        def body(kk, carry):
            @pl.when(kk != k)
            def _():
                action(kk)

            return carry

        lax.fori_loop(0, count, body, 0)

    def piece(r, b, kk):
        chunk = grads[r][5]
        return grads[r][0].at[b, pl.ds(pl.multiple_of(kk * chunk, 16), chunk)]

    def to_owner(r, b, kk):
        return pltpu.make_async_remote_copy(
            src_ref=piece(r, b, kk), dst_ref=grads[r][1].at[b, k],
            send_sem=grads[r][7].at[b, kk], recv_sem=grads[r][8].at[b, k],
            device_id=(s, kk), device_id_type=MESH,
        )

    def from_peer(r, b, kk):
        slot = grads[r][1].at[b, kk]
        return pltpu.make_async_remote_copy(
            src_ref=slot, dst_ref=slot,
            send_sem=grads[r][7].at[b, 0], recv_sem=grads[r][8].at[b, kk],
            device_id=(s, kk), device_id_type=MESH,
        )

    def to_section(r, b, slot):
        return pltpu.make_async_remote_copy(
            src_ref=grads[r][2].at[b], dst_ref=grads[r][3].at[slot],
            send_sem=grads[r][9].at[b], recv_sem=grads[r][10].at[slot],
            device_id=(b, k), device_id_type=MESH,
        )

    def final_copy(r, kk, slot):
        return pltpu.make_async_remote_copy(
            src_ref=grads[r][4].at[slot], dst_ref=grads[r][4].at[slot],
            send_sem=grads[r][11].at[kk], recv_sem=grads[r][12].at[slot],
            device_id=(s, kk), device_id_type=MESH,
        )

    def scatter(r, b):
        others(counts[r], lambda kk: to_owner(r, b, kk).start())

    def owner_sum(r, b):
        G, RS, PART, SG = grads[r][:4]
        chunk = chunks[r]

        @pl.when(k < counts[r])
        def _():
            RS[b, k] = G[b, pl.ds(pl.multiple_of(k * chunk, 16), chunk)]
            others(n, lambda kk: from_peer(r, b, kk).wait_recv())
            total = lax.fori_loop(
                0, n, lambda i, acc: acc + RS[b, i].astype(jnp.float32),
                jnp.zeros((chunk, 128), jnp.float32),
            ).astype(bf)

            @pl.when(b == s)
            def _():
                SG[s] = total

            @pl.when(b != s)
            def _():
                PART[b] = total
                to_section(r, b, s).start()

    def late_grads(b):
        red = t_mm(DD1[...], acts[b]).astype(bf)
        G1[b, :64] = red[:, :128]
        G1[b, 64:] = red[:, 128:]
        scatter(1, b)

    def backward(step, carry):
        b = blocks - 1 - step
        par = lax.rem(step + blocks, 2)
        scale = NS[b]
        d3 = dins[b + 1].astype(jnp.float32) * D3[b]
        DD3[...] = d3
        e3 = (d3 * scale[:, 128:]).astype(bf)
        d2 = (mm_t(e3, W3[b]) * D2[b]).astype(bf)
        zero = jnp.zeros((SIDE, 64), bf)
        d2cat = jnp.concatenate(
            [
                jnp.concatenate([d2, zero, zero], axis=0),
                jnp.concatenate([zero, d2, zero], axis=0),
                jnp.concatenate([zero, zero, d2], axis=0),
            ],
            axis=1,
        )
        dcat = mm(d2cat, WC[b])
        sides = jnp.concatenate([dcat[:, :64], dcat[:, 128:]], axis=0).astype(bf)
        drim = mm(rim_t_ref[...], sides)
        mid = dcat[:, 64:128]
        faces = jnp.concatenate(
            [drim[:SIDE] + mid[:SIDE], drim[SIDE : 2 * SIDE] + mid[SIDE + PIX :], drim[2 * SIDE :]],
            axis=0,
        )
        start_exchange(par, faces.astype(bf))
        dmid = (mm(inner_t_ref[...], sides) + mid[SIDE : SIDE + PIX]).astype(bf)
        taps = t_mm(d2cat, CAT[b]).astype(bf)
        G0[b, :192] = taps[:, :128]
        G0[b, 192:288] = jnp.concatenate([taps[:96, 128:], taps[96:, 128:]], axis=1)
        expand = t_mm(H2[b], e3).astype(bf)
        G0[b, 288:352] = expand[:, :128]
        G0[b, 352:416] = expand[:, 128:]
        spare = counts[0] * chunks[0] - REGIONS[0]
        if spare:
            G0[b, REGIONS[0] :] = jnp.zeros((spare, 128), bf)
        scatter(0, b)
        sent(1 - par)

        @pl.when(step == 0)
        def _():
            send_result(0, blocks - 1, out_ref, acts.at[blocks])

        @pl.when(step > 0)
        def _():
            send_result(1, b + 1, din_ref, dins.at[b + 1])
            late_grads(b + 1)
            owner_sum(0, b + 1)

        @pl.when(step > 1)
        def _():
            owner_sum(1, b + 2)

        got = end_exchange(par)
        dh1 = dmid.astype(jnp.float32) + mm(
            face_t_ref[...], jnp.concatenate(got, axis=0)
        )
        d1 = (dh1 * D1[b]).astype(bf)
        DD1[...] = d1
        dins[b] = (DD3[...] + mm(d1, W1[b])).astype(bf)
        return carry

    lax.fori_loop(0, blocks, backward, 0)
    late_grads(0)
    send_result(1, 0, din_ref, dins.at[0], (0,))
    owner_sum(1, 1)
    sent((2 * blocks - 1) % 2)

    for r in (0, 1):
        owner_sum(r, 0)
    send_result(1, 0, din_ref, dins.at[0], (1,))
    for r in (0, 1):
        SG, FIN = grads[r][3:5]

        @pl.when(k < counts[r])
        def _():
            for ss in range(blocks):
                @pl.when(s != ss)
                def _():
                    to_section(r, ss, ss).wait_recv()

            FIN[k] = sum(SG[ss].astype(jnp.float32) for ss in range(blocks)).astype(bf)
            others(n, lambda kk: final_copy(r, kk, k).start())

    for r in (0, 1):
        others(counts[r], lambda kk: final_copy(r, kk, kk).wait_recv())
    done = FIN0[...].reshape(counts[0] * chunks[0], 128).astype(jnp.float32)
    red = FIN1[...].reshape(REGIONS[1], 128).astype(jnp.float32)
    right = jnp.concatenate([done[192:288, :64], done[192:288, 64:]], axis=0)
    for dy in range(3):
        span = slice(64 * dy, 64 * dy + 64)
        gt_ref[0, :, 192 * dy : 192 * dy + 192] = jnp.concatenate(
            [done[span], right[span]], axis=1
        )
    ge_ref[0, :, :128] = done[288:352]
    ge_ref[0, :, 128:] = done[352:416]
    gr_ref[0, :, :128] = red[:64]
    gr_ref[0, :, 128:] = red[64:]

    for r in (0, 1):
        for b in range(blocks):
            others(counts[r], lambda kk: to_owner(r, b, kk).wait_send())

        @pl.when(k < counts[r])
        def _():
            others(n, lambda kk: final_copy(r, kk, k).wait_send())
            for ss in range(blocks):
                @pl.when(s != ss)
                def _():
                    to_section(r, ss, ss).wait_send()

    for ss in range(blocks):
        @pl.when(s != ss)
        def _():
            for i in range(len(weights)):
                weight_copy(i, ss, ss).wait_send()
            for which, ref, held in ((0, out_ref, acts.at[ss + 1]), (1, din_ref, dins.at[ss])):
                for half in (0, 1):
                    result_copy(which, ss, ref, held, half, ss).wait()

    result_local(0, out_ref, acts.at[s + 1]).wait()
    result_local(1, din_ref, dins.at[s]).wait()


def copy_out(*refs):
    held, load, store = refs[10:15], refs[15], refs[16]
    pieces = [
        (refs[i].at[part], held[i].at[part], refs[5 + i].at[part])
        for i in range(5)
        for part in range(refs[i].shape[0])
    ]
    loads = [pltpu.make_async_copy(p[0], p[1], load.at[i]) for i, p in enumerate(pieces)]
    stores = [pltpu.make_async_copy(p[1], p[2], store.at[i]) for i, p in enumerate(pieces)]
    for copy in loads:
        copy.start()
    for before, after in zip(loads, stores):
        before.wait()
        after.start()
    for copy in stores:
        copy.wait()


def on_device(
    features, out_cotangent, w_reduce, w_taps, w_expand, norm_scale, norm_shift, owner, neighbours
):
    blocks = lax.axis_size("section")
    n = lax.axis_size("tile")
    slots, side, _, chans = features.shape
    bf, f32 = jnp.bfloat16, jnp.float32
    chunks = [16 * max(1, -(-rows // (16 * n))) for rows in REGIONS]
    counts = [-(-rows // chunk) for rows, chunk in zip(REGIONS, chunks)]
    shift, face = shift_matrices()
    inner = shift[:, SIDE : SIDE + PIX]
    rim = np.concatenate([shift[:, :SIDE], shift[:, SIDE + PIX :]], axis=1)
    consts = [jnp.asarray(m, bf) for m in (inner, rim, inner.T, rim.T, face, face.T)]
    vmem = pl.BlockSpec(memory_space=pltpu.VMEM)
    smem = pl.BlockSpec(memory_space=pltpu.SMEM)
    anyw = pl.BlockSpec(memory_space=pl.ANY)
    hbm = pl.BlockSpec(memory_space=pltpu.HBM)
    dma = pltpu.SemaphoreType.DMA
    spots = SPAN * blocks
    results = pl.pallas_call(
        partial(kernel, n, blocks, chunks, counts),
        out_shape=(
            jax.ShapeDtypeStruct((slots, PIX, chans), bf),
            jax.ShapeDtypeStruct((slots, PIX, chans), bf),
            jax.ShapeDtypeStruct((1, 64, 256), f32),
            jax.ShapeDtypeStruct((1, 64, 576), f32),
            jax.ShapeDtypeStruct((1, 64, 256), f32),
        ),
        in_specs=[smem] * 2 + [hbm] * 13,
        out_specs=[anyw] * 2 + [vmem] * 3,
        scratch_shapes=[
            pltpu.SMEM((spots,), jnp.int32),
            *[pltpu.VMEM(m.shape, bf) for m in consts],
            pltpu.VMEM((blocks + 1, PIX, chans), bf),
            pltpu.VMEM((blocks + 1, PIX, chans), bf),
            pltpu.VMEM((blocks, 64, 256), bf),
            pltpu.VMEM((blocks, 64, 576), bf),
            pltpu.VMEM((blocks, 64, 256), bf),
            pltpu.VMEM((blocks, 192, 192), bf),
            pltpu.VMEM((blocks, 1, 384), f32),
            pltpu.VMEM((blocks, 1, 384), f32),
            pltpu.VMEM((blocks, PIX, 64), f32),
            pltpu.VMEM((blocks, PIX, 64), f32),
            pltpu.VMEM((blocks, PIX, chans), f32),
            pltpu.VMEM((PIX, 64), f32),
            pltpu.VMEM((PIX, chans), f32),
            pltpu.VMEM((blocks, EXT, 192), bf),
            pltpu.VMEM((blocks, PIX, 64), bf),
            pltpu.VMEM((PIX, 64), bf),
            pltpu.VMEM((PIX, chans), f32),
            pltpu.VMEM((4, SIDE, 128), bf),
            pltpu.VMEM((2, spots, SIDE, 128), bf),
            pltpu.VMEM((2, spots, SIDE, 128), bf),
            pltpu.VMEM((spots, SIDE, 128), bf),
            *[pltpu.VMEM((blocks, c * m, 128), bf) for c, m in zip(chunks, counts)],
            *[pltpu.VMEM((blocks, n, c, 128), bf) for c in chunks],
            *[pltpu.VMEM((blocks, c, 128), bf) for c in chunks],
            *[pltpu.VMEM((blocks, c, 128), bf) for c in chunks],
            *[pltpu.VMEM((m, c, 128), bf) for c, m in zip(chunks, counts)],
            dma((2,)), dma((6,)), dma((5,)), dma((5, blocks)), dma((5, blocks)),
            dma((2, spots)), dma((2, spots)),
            dma((2, blocks, 2)), dma((2, blocks, 2)), dma((2,)),
            *[
                dma(shape)
                for m in counts
                for shape in ((blocks, m), (blocks, n), (blocks,), (blocks,), (n,), (m,))
            ],
        ],
        compiler_params=pltpu.CompilerParams(
            collective_id=0, has_side_effects=True, vmem_limit_bytes=60 * 1024 * 1024
        ),
        name="residual_blocks",
    )(
        owner, neighbours.T,
        features.reshape(slots, PIX, chans), out_cotangent.reshape(slots, PIX, chans),
        jnp.swapaxes(w_reduce, 1, 2), jnp.swapaxes(w_taps, 1, 2), w_expand, norm_scale, norm_shift,
        *consts,
    )
    results = pl.pallas_call(
        copy_out,
        out_shape=tuple(jax.ShapeDtypeStruct(r.shape, r.dtype) for r in results),
        in_specs=[anyw] * 5,
        out_specs=[anyw] * 5,
        scratch_shapes=[
            *[pltpu.VMEM(r.shape, r.dtype) for r in results],
            dma((2 * slots + 3,)), dma((2 * slots + 3,)),
        ],
        name="copy_out",
    )(*results)
    shape = (1, slots, side, side, chans)
    return (
        results[0].reshape(shape), results[1].reshape(shape),
        jnp.swapaxes(results[2], 1, 2), jnp.swapaxes(results[3], 1, 2), results[4],
    )


def solution(mesh):
    return jax.shard_map(
        on_device,
        mesh=mesh,
        in_specs=(
            P("tile", None, None, None),
            P("tile", None, None, None),
            P("section", None, None),
            P("section", None, None),
            P("section", None, None),
            P("section", None),
            P("section", None),
            P(),
            P(),
        ),
        out_specs=(
            P("section", "tile", None, None, None),
            P("section", "tile", None, None, None),
            P("section", None, None),
            P("section", None, None),
            P("section", None, None),
        ),
        check_vma=False,
    )
```

```python
from functools import partial

import jax
import jax.numpy as jnp
import numpy as np
from jax import lax
from jax.experimental import pallas as pl
from jax.experimental.pallas import tpu as pltpu
from jax.sharding import PartitionSpec as P

REACH = 3
SPAN = 2 * REACH + 1
MESH = pl.DeviceIdType.MESH
SIDE = 16
PIX = SIDE * SIDE
EXT = PIX + 2 * SIDE
FULL = EXT + 2 * SIDE
REGIONS = (416, 128)


def shift_matrices():
    left = np.zeros((EXT, FULL), np.float32)
    right = np.zeros((EXT, FULL), np.float32)
    for r in range(EXT):
        y, x = r // SIDE - 1, r % SIDE
        inside = 0 <= y < SIDE
        if x > 0:
            left[r, r - 1] = 1
        elif inside:
            left[r, EXT + y] = 1
        if x < SIDE - 1:
            right[r, r + 1] = 1
        elif inside:
            right[r, EXT + SIDE + y] = 1
    face = np.zeros((4 * SIDE, PIX), np.float32)
    for i in range(SIDE):
        face[i, i] = 1
        face[SIDE + i, PIX - SIDE + i] = 1
        face[2 * SIDE + i, SIDE * i] = 1
        face[3 * SIDE + i, SIDE * i + SIDE - 1] = 1
    return np.concatenate([left, right]), face


def sigmoid(v):
    return 0.5 * jnp.tanh(0.5 * v) + 0.5


def mm(left, right):
    return jnp.dot(left, right, preferred_element_type=jnp.float32)


def mm_t(left, right):
    return lax.dot_general(
        left, right, (((1,), (1,)), ((), ())), preferred_element_type=jnp.float32
    )


def t_mm(left, right):
    return lax.dot_general(
        left, right, (((0,), (0,)), ((), ())), preferred_element_type=jnp.float32
    )


def kernel(
    n, blocks, chunks, counts,
    owner_ref, near_ref, feat_ref, cot_ref, w1_ref, wt_ref, w3_ref, sc_ref, sh_ref,
    inner_in, rim_in, inner_t_in, rim_t_in, face_in, face_t_in,
    out_ref, din_ref, gr_ref, gt_ref, ge_ref,
    sel, inner_ref, rim_ref, inner_t_ref, rim_t_ref, face_ref, face_t_ref, acts, dins, W1, WT, W3, WC, NS, NT,
    D1, D2, D3, pre2_s, pre3_s, CAT, H2, DD1, DD3, F, SEND, RECV, HELD, G0, G1, RS0, RS1, PART0, PART1, SG0, SG1, FIN0, FIN1,
    load_sem, const_sem, wl_sem, ws_sem, wr_sem, xs_sem, xr_sem,
    os_sem, or_sem, ol_sem, *grad_sems,
):
    s = lax.axis_index("section")
    k = lax.axis_index("tile")
    lo = jnp.maximum(k - REACH, 0)
    hi = jnp.minimum(k + REACH + 1, n)
    bf = jnp.bfloat16

    feat_copy = pltpu.make_async_copy(feat_ref.at[s], acts.at[0], load_sem.at[0])
    cot_copy = pltpu.make_async_copy(cot_ref.at[s], dins.at[blocks], load_sem.at[1])
    const_copies = [
        pltpu.make_async_copy(src, dst, const_sem.at[i])
        for i, (src, dst) in enumerate([
            (face_in, face_ref), (inner_in, inner_ref), (rim_in, rim_ref),
            (inner_t_in, inner_t_ref), (rim_t_in, rim_t_ref), (face_t_in, face_t_ref),
        ])
    ]
    feat_copy.start()
    weights = [
        (w1_ref.at[0], W1), (sc_ref, NS), (sh_ref, NT), (wt_ref.at[0], WT), (w3_ref.at[0], W3)
    ]
    for i, (src, dst) in enumerate(weights):
        pltpu.make_async_copy(src, dst.at[s], wl_sem.at[i]).start()
    for copy in const_copies:
        copy.start()
    cot_copy.start()

    barrier = pltpu.get_barrier_semaphore()

    def greet(kk, total):
        near = jnp.logical_and(kk >= lo, kk < hi)
        for ss in range(blocks):
            go = jnp.logical_and(
                jnp.logical_or(near, s == ss), jnp.logical_not(jnp.logical_and(s == ss, kk == k))
            )

            @pl.when(go)
            def _():
                pl.semaphore_signal(barrier, inc=1, device_id=(ss, kk), device_id_type=MESH)

        return total

    lax.fori_loop(0, n, greet, 0)
    slot = k * blocks + s
    tiles = owner_ref.shape[0]
    tile = lax.fori_loop(
        0, tiles, lambda i, acc: jnp.where(owner_ref[i] == slot, i, acc), jnp.int32(0)
    )
    places, valids = [], []
    for j in range(4):
        near = near_ref[j, tile]
        valid = near >= 0
        where = owner_ref[jnp.where(valid, near, 0)]
        hop = lax.rem(where % blocks - s + blocks, blocks)
        place = (where // blocks - k + REACH) * blocks + hop
        place = jnp.where(valid, place, 0)
        places.append(jnp.clip(place, 0, SPAN * blocks - 1))
        valids.append(valid)
    for i in range(SPAN * blocks):
        pick = jnp.int32(0)
        for j in range(1, 4):
            pick = jnp.where(jnp.logical_and(valids[j], places[j] == i), j, pick)
        sel[i] = pick

    pl.semaphore_wait(barrier, (hi - lo) * (blocks - 1) + n - 1)

    def weight_copy(i, target, slot):
        src, dst = weights[i]
        return pltpu.make_async_remote_copy(
            src_ref=src, dst_ref=dst.at[slot],
            send_sem=ws_sem.at[i, target], recv_sem=wr_sem.at[i, slot],
            device_id=(target, k), device_id_type=MESH,
        )

    def send_weights():
        for i in range(len(weights)):
            for target in range(blocks):
                @pl.when(s != target)
                def _():
                    weight_copy(i, target, s).start()

    @pl.when(s == 0)
    def _():
        send_weights()

    def partners():
        for far in sorted(range(-REACH, REACH + 1), key=lambda o: -abs(o)):
            yield far, [hop for hop in range(blocks) if far or hop]

    def exchange_copy(par, far, hop):
        theirs = (far + REACH) * blocks + hop
        mine = (REACH - far) * blocks + (blocks - hop) % blocks
        return pltpu.make_async_remote_copy(
            src_ref=SEND.at[par, theirs], dst_ref=RECV.at[par, mine],
            send_sem=xs_sem.at[par, theirs], recv_sem=xr_sem.at[par, mine],
            device_id=(lax.rem(s + hop, blocks), k + far), device_id_type=MESH,
        )

    def each_partner(action):
        for far, hops in partners():
            def body():
                for hop in hops:
                    action(far, hop)

            if far:
                pl.when(jnp.logical_and(k + far >= 0, k + far < n))(body)
            else:
                body()

    def sent(par):
        each_partner(lambda far, hop: exchange_copy(par, far, hop).wait_send())

    def start_exchange(par, faces):
        F[...] = jnp.concatenate([faces, faces], axis=1).reshape(4, SIDE, 128)
        for i in range(SPAN * blocks):
            SEND[par, i] = F[sel[i]]
        each_partner(lambda far, hop: exchange_copy(par, far, hop).start())

    def end_exchange(par):
        each_partner(lambda far, hop: exchange_copy(par, -far, -hop % blocks).wait_recv())
        HELD[...] = RECV[par]
        got = []
        for j in range(4):
            face = HELD[places[j]][:, :64]
            got.append(jnp.where(valids[j], face.astype(jnp.float32), 0.0).astype(bf))
        return got

    def result_copy(which, b, ref, src, half, slot):
        rows = pl.ds(half * (PIX // 2), PIX // 2)
        return pltpu.make_async_remote_copy(
            src_ref=src.at[rows], dst_ref=ref.at[slot, rows],
            send_sem=os_sem.at[which, b, half], recv_sem=or_sem.at[which, slot, half],
            device_id=(b, k), device_id_type=MESH,
        )

    def result_local(which, ref, src):
        return pltpu.make_async_copy(src, ref.at[s], ol_sem.at[which])

    def send_result(which, b, ref, src, halves=(0, 1)):
        @pl.when(b != s)
        def _():
            for half in halves:
                result_copy(which, b, ref, src, half, s).start()

        if 0 in halves:
            @pl.when(b == s)
            def _():
                result_local(which, ref, src).start()

    def derivative(v):
        sig = sigmoid(v)
        return sig * (1.0 + v * (1.0 - sig))

    def tail_derivatives(b):
        D2[b] = derivative(pre2_s[...]) * NS[b][:, 64:128]
        D3[b] = derivative(pre3_s[...])

    for i, (src, dst) in enumerate(weights):
        pltpu.make_async_copy(src, dst.at[s], wl_sem.at[i]).wait()
    feat_copy.wait()
    const_copies[0].wait()

    def forward(b, carry):
        par = lax.rem(b, 2)

        @pl.when(b != s)
        def _():
            for i in range(len(weights)):
                weight_copy(i, b, b).wait_recv()

        a = acts[b]
        scale = NS[b]
        shift = NT[b]
        pre1 = mm_t(a, W1[b]) * scale[:, :64] + shift[:, :64]
        sig = sigmoid(pre1)
        h1 = (pre1 * sig).astype(bf)
        start_exchange(par, mm(face_ref[...], h1).astype(bf))

        @pl.when(b > 0)
        def _():
            sent(1 - par)
            send_result(0, b - 1, out_ref, acts.at[b])
            tail_derivatives(b - 1)

        @pl.when(b == 0)
        def _():
            for copy in const_copies[1:]:
                copy.wait()

        @pl.when(jnp.logical_and(b == 0, s != 0))
        def _():
            send_weights()

        D1[b] = sig * (1.0 + pre1 * (1.0 - sig)) * scale[:, :64]
        taps = WT[b]
        WC[b] = jnp.concatenate([taps[:, :192], taps[:, 192:384], taps[:, 384:]], axis=0)
        moved = mm(inner_ref[...], h1)

        got = end_exchange(par)
        full = jnp.concatenate([got[0], h1, got[1]], axis=0)
        moved = (moved + mm(rim_ref[...], jnp.concatenate(got, axis=0))).astype(bf)
        cat = jnp.concatenate([moved[:EXT], full, moved[EXT:]], axis=1)
        CAT[b] = cat
        rows = mm_t(cat, WC[b])
        pre2 = (
            rows[:PIX, :64] + rows[SIDE : SIDE + PIX, 64:128] + rows[2 * SIDE :, 128:]
        )
        pre2 = pre2 * scale[:, 64:128] + shift[:, 64:128]
        pre2_s[...] = pre2
        h2 = (pre2 * sigmoid(pre2)).astype(bf)
        H2[b] = h2
        pre3 = a.astype(jnp.float32) + mm(h2, W3[b]) * scale[:, 128:] + shift[:, 128:]
        pre3_s[...] = pre3
        acts[b + 1] = (pre3 * sigmoid(pre3)).astype(bf)
        return carry

    lax.fori_loop(0, blocks, forward, 0)
    tail_derivatives(blocks - 1)
    cot_copy.wait()

    grads = [
        (G0, RS0, PART0, SG0, FIN0, chunks[0], counts[0]) + grad_sems[:6],
        (G1, RS1, PART1, SG1, FIN1, chunks[1], counts[1]) + grad_sems[6:],
    ]

    def others(count, action):
        def body(kk, carry):
            @pl.when(kk != k)
            def _():
                action(kk)

            return carry

        lax.fori_loop(0, count, body, 0)

    def piece(r, b, kk):
        chunk = grads[r][5]
        return grads[r][0].at[b, pl.ds(pl.multiple_of(kk * chunk, 16), chunk)]

    def to_owner(r, b, kk):
        return pltpu.make_async_remote_copy(
            src_ref=piece(r, b, kk), dst_ref=grads[r][1].at[b, k],
            send_sem=grads[r][7].at[b, kk], recv_sem=grads[r][8].at[b, k],
            device_id=(s, kk), device_id_type=MESH,
        )

    def from_peer(r, b, kk):
        slot = grads[r][1].at[b, kk]
        return pltpu.make_async_remote_copy(
            src_ref=slot, dst_ref=slot,
            send_sem=grads[r][7].at[b, 0], recv_sem=grads[r][8].at[b, kk],
            device_id=(s, kk), device_id_type=MESH,
        )

    def to_section(r, b, slot):
        return pltpu.make_async_remote_copy(
            src_ref=grads[r][2].at[b], dst_ref=grads[r][3].at[slot],
            send_sem=grads[r][9].at[b], recv_sem=grads[r][10].at[slot],
            device_id=(b, k), device_id_type=MESH,
        )

    def final_copy(r, kk, slot):
        return pltpu.make_async_remote_copy(
            src_ref=grads[r][4].at[slot], dst_ref=grads[r][4].at[slot],
            send_sem=grads[r][11].at[kk], recv_sem=grads[r][12].at[slot],
            device_id=(s, kk), device_id_type=MESH,
        )

    def scatter(r, b):
        others(counts[r], lambda kk: to_owner(r, b, kk).start())

    def owner_sum(r, b):
        G, RS, PART, SG = grads[r][:4]
        chunk = chunks[r]

        @pl.when(k < counts[r])
        def _():
            RS[b, k] = G[b, pl.ds(pl.multiple_of(k * chunk, 16), chunk)]
            others(n, lambda kk: from_peer(r, b, kk).wait_recv())
            total = lax.fori_loop(
                0, n, lambda i, acc: acc + RS[b, i].astype(jnp.float32),
                jnp.zeros((chunk, 128), jnp.float32),
            ).astype(bf)

            @pl.when(b == s)
            def _():
                SG[s] = total

            @pl.when(b != s)
            def _():
                PART[b] = total
                to_section(r, b, s).start()

    def late_grads(b):
        red = t_mm(DD1[...], acts[b]).astype(bf)
        G1[b, :64] = red[:, :128]
        G1[b, 64:] = red[:, 128:]
        scatter(1, b)

    def backward(step, carry):
        b = blocks - 1 - step
        par = lax.rem(step + blocks, 2)
        scale = NS[b]
        d3 = dins[b + 1].astype(jnp.float32) * D3[b]
        DD3[...] = d3
        e3 = (d3 * scale[:, 128:]).astype(bf)
        d2 = (mm_t(e3, W3[b]) * D2[b]).astype(bf)
        zero = jnp.zeros((SIDE, 64), bf)
        d2cat = jnp.concatenate(
            [
                jnp.concatenate([d2, zero, zero], axis=0),
                jnp.concatenate([zero, d2, zero], axis=0),
                jnp.concatenate([zero, zero, d2], axis=0),
            ],
            axis=1,
        )
        dcat = mm(d2cat, WC[b])
        sides = jnp.concatenate([dcat[:, :64], dcat[:, 128:]], axis=0).astype(bf)
        drim = mm(rim_t_ref[...], sides)
        mid = dcat[:, 64:128]
        faces = jnp.concatenate(
            [drim[:SIDE] + mid[:SIDE], drim[SIDE : 2 * SIDE] + mid[SIDE + PIX :], drim[2 * SIDE :]],
            axis=0,
        )
        start_exchange(par, faces.astype(bf))
        dmid = (mm(inner_t_ref[...], sides) + mid[SIDE : SIDE + PIX]).astype(bf)
        taps = t_mm(d2cat, CAT[b]).astype(bf)
        G0[b, :192] = taps[:, :128]
        G0[b, 192:288] = jnp.concatenate([taps[:96, 128:], taps[96:, 128:]], axis=1)
        expand = t_mm(H2[b], e3).astype(bf)
        G0[b, 288:352] = expand[:, :128]
        G0[b, 352:416] = expand[:, 128:]
        spare = counts[0] * chunks[0] - REGIONS[0]
        if spare:
            G0[b, REGIONS[0] :] = jnp.zeros((spare, 128), bf)
        scatter(0, b)
        sent(1 - par)

        @pl.when(step == 0)
        def _():
            send_result(0, blocks - 1, out_ref, acts.at[blocks])

        @pl.when(step > 0)
        def _():
            send_result(1, b + 1, din_ref, dins.at[b + 1])
            late_grads(b + 1)
            owner_sum(0, b + 1)

        @pl.when(step > 1)
        def _():
            owner_sum(1, b + 2)

        got = end_exchange(par)
        dh1 = dmid.astype(jnp.float32) + mm(
            face_t_ref[...], jnp.concatenate(got, axis=0)
        )
        d1 = (dh1 * D1[b]).astype(bf)
        DD1[...] = d1
        dins[b] = (DD3[...] + mm(d1, W1[b])).astype(bf)
        return carry

    lax.fori_loop(0, blocks, backward, 0)
    late_grads(0)
    send_result(1, 0, din_ref, dins.at[0], (0,))
    owner_sum(1, 1)
    sent((2 * blocks - 1) % 2)

    for r in (0, 1):
        owner_sum(r, 0)
    send_result(1, 0, din_ref, dins.at[0], (1,))
    for r in (0, 1):
        SG, FIN = grads[r][3:5]

        @pl.when(k < counts[r])
        def _():
            for ss in range(blocks):
                @pl.when(s != ss)
                def _():
                    to_section(r, ss, ss).wait_recv()

            FIN[k] = sum(SG[ss].astype(jnp.float32) for ss in range(blocks)).astype(bf)
            others(n, lambda kk: final_copy(r, kk, k).start())

    for r in (0, 1):
        others(counts[r], lambda kk: final_copy(r, kk, kk).wait_recv())
    done = FIN0[...].reshape(counts[0] * chunks[0], 128).astype(jnp.float32)
    red = FIN1[...].reshape(REGIONS[1], 128).astype(jnp.float32)
    right = jnp.concatenate([done[192:288, :64], done[192:288, 64:]], axis=0)
    for dy in range(3):
        span = slice(64 * dy, 64 * dy + 64)
        gt_ref[0, :, 192 * dy : 192 * dy + 192] = jnp.concatenate(
            [done[span], right[span]], axis=1
        )
    ge_ref[0, :, :128] = done[288:352]
    ge_ref[0, :, 128:] = done[352:416]
    gr_ref[0, :, :128] = red[:64]
    gr_ref[0, :, 128:] = red[64:]

    for r in (0, 1):
        for b in range(blocks):
            others(counts[r], lambda kk: to_owner(r, b, kk).wait_send())

        @pl.when(k < counts[r])
        def _():
            others(n, lambda kk: final_copy(r, kk, k).wait_send())
            for ss in range(blocks):
                @pl.when(s != ss)
                def _():
                    to_section(r, ss, ss).wait_send()

    for ss in range(blocks):
        @pl.when(s != ss)
        def _():
            for i in range(len(weights)):
                weight_copy(i, ss, ss).wait_send()
            for which, ref, held in ((0, out_ref, acts.at[ss + 1]), (1, din_ref, dins.at[ss])):
                for half in (0, 1):
                    result_copy(which, ss, ref, held, half, ss).wait()

    result_local(0, out_ref, acts.at[s + 1]).wait()
    result_local(1, din_ref, dins.at[s]).wait()


def copy_out(*refs):
    held, load, store = refs[10:15], refs[15], refs[16]
    pieces = [
        (refs[i].at[part], held[i].at[part], refs[5 + i].at[part])
        for i in range(5)
        for part in range(refs[i].shape[0])
    ]
    loads = [pltpu.make_async_copy(p[0], p[1], load.at[i]) for i, p in enumerate(pieces)]
    stores = [pltpu.make_async_copy(p[1], p[2], store.at[i]) for i, p in enumerate(pieces)]
    for copy in loads:
        copy.start()
    for before, after in zip(loads, stores):
        before.wait()
        after.start()
    for copy in stores:
        copy.wait()


def on_device(
    features, out_cotangent, w_reduce, w_taps, w_expand, norm_scale, norm_shift, owner, neighbours
):
    blocks = lax.axis_size("section")
    n = lax.axis_size("tile")
    slots, side, _, chans = features.shape
    bf, f32 = jnp.bfloat16, jnp.float32
    chunks = [16 * max(1, -(-rows // (16 * n))) for rows in REGIONS]
    counts = [-(-rows // chunk) for rows, chunk in zip(REGIONS, chunks)]
    shift, face = shift_matrices()
    inner = shift[:, SIDE : SIDE + PIX]
    rim = np.concatenate([shift[:, :SIDE], shift[:, SIDE + PIX :]], axis=1)
    consts = [jnp.asarray(m, bf) for m in (inner, rim, inner.T, rim.T, face, face.T)]
    vmem = pl.BlockSpec(memory_space=pltpu.VMEM)
    smem = pl.BlockSpec(memory_space=pltpu.SMEM)
    anyw = pl.BlockSpec(memory_space=pl.ANY)
    hbm = pl.BlockSpec(memory_space=pltpu.HBM)
    dma = pltpu.SemaphoreType.DMA
    spots = SPAN * blocks
    results = pl.pallas_call(
        partial(kernel, n, blocks, chunks, counts),
        out_shape=(
            jax.ShapeDtypeStruct((slots, PIX, chans), bf),
            jax.ShapeDtypeStruct((slots, PIX, chans), bf),
            jax.ShapeDtypeStruct((1, 64, 256), f32),
            jax.ShapeDtypeStruct((1, 64, 576), f32),
            jax.ShapeDtypeStruct((1, 64, 256), f32),
        ),
        in_specs=[smem] * 2 + [hbm] * 13,
        out_specs=[anyw] * 2 + [vmem] * 3,
        scratch_shapes=[
            pltpu.SMEM((spots,), jnp.int32),
            *[pltpu.VMEM(m.shape, bf) for m in consts],
            pltpu.VMEM((blocks + 1, PIX, chans), bf),
            pltpu.VMEM((blocks + 1, PIX, chans), bf),
            pltpu.VMEM((blocks, 64, 256), bf),
            pltpu.VMEM((blocks, 64, 576), bf),
            pltpu.VMEM((blocks, 64, 256), bf),
            pltpu.VMEM((blocks, 192, 192), bf),
            pltpu.VMEM((blocks, 1, 384), f32),
            pltpu.VMEM((blocks, 1, 384), f32),
            pltpu.VMEM((blocks, PIX, 64), f32),
            pltpu.VMEM((blocks, PIX, 64), f32),
            pltpu.VMEM((blocks, PIX, chans), f32),
            pltpu.VMEM((PIX, 64), f32),
            pltpu.VMEM((PIX, chans), f32),
            pltpu.VMEM((blocks, EXT, 192), bf),
            pltpu.VMEM((blocks, PIX, 64), bf),
            pltpu.VMEM((PIX, 64), bf),
            pltpu.VMEM((PIX, chans), f32),
            pltpu.VMEM((4, SIDE, 128), bf),
            pltpu.VMEM((2, spots, SIDE, 128), bf),
            pltpu.VMEM((2, spots, SIDE, 128), bf),
            pltpu.VMEM((spots, SIDE, 128), bf),
            *[pltpu.VMEM((blocks, c * m, 128), bf) for c, m in zip(chunks, counts)],
            *[pltpu.VMEM((blocks, n, c, 128), bf) for c in chunks],
            *[pltpu.VMEM((blocks, c, 128), bf) for c in chunks],
            *[pltpu.VMEM((blocks, c, 128), bf) for c in chunks],
            *[pltpu.VMEM((m, c, 128), bf) for c, m in zip(chunks, counts)],
            dma((2,)), dma((6,)), dma((5,)), dma((5, blocks)), dma((5, blocks)),
            dma((2, spots)), dma((2, spots)),
            dma((2, blocks, 2)), dma((2, blocks, 2)), dma((2,)),
            *[
                dma(shape)
                for m in counts
                for shape in ((blocks, m), (blocks, n), (blocks,), (blocks,), (n,), (m,))
            ],
        ],
        compiler_params=pltpu.CompilerParams(
            collective_id=0, has_side_effects=True, vmem_limit_bytes=60 * 1024 * 1024
        ),
        name="residual_blocks",
    )(
        owner, neighbours.T,
        features.reshape(slots, PIX, chans), out_cotangent.reshape(slots, PIX, chans),
        jnp.swapaxes(w_reduce, 1, 2), jnp.swapaxes(w_taps, 1, 2), w_expand, norm_scale, norm_shift,
        *consts,
    )
    results = pl.pallas_call(
        copy_out,
        out_shape=tuple(jax.ShapeDtypeStruct(r.shape, r.dtype) for r in results),
        in_specs=[anyw] * 5,
        out_specs=[anyw] * 5,
        scratch_shapes=[
            *[pltpu.VMEM(r.shape, r.dtype) for r in results],
            dma((2 * slots + 3,)), dma((2 * slots + 3,)),
        ],
        name="copy_out",
    )(*results)
    shape = (1, slots, side, side, chans)
    return (
        results[0].reshape(shape), results[1].reshape(shape),
        jnp.swapaxes(results[2], 1, 2), jnp.swapaxes(results[3], 1, 2), results[4],
    )


def solution(mesh):
    return jax.shard_map(
        on_device,
        mesh=mesh,
        in_specs=(
            P("tile", None, None, None),
            P("tile", None, None, None),
            P("section", None, None),
            P("section", None, None),
            P("section", None, None),
            P("section", None),
            P("section", None),
            P(),
            P(),
        ),
        out_specs=(
            P("section", "tile", None, None, None),
            P("section", "tile", None, None, None),
            P("section", None, None),
            P("section", None, None),
            P("section", None, None),
        ),
        check_vma=False,
    )
```
